512 devices in a mesh: dp: 32 (over z, core), mp: 16 (over x, y).
Axes of the slice: x: 4, y: 4, z: 16, core: 2. Of those that a mesh axis runs over, the one named last changes fastest.
Arguments:
- activations: bfloat16 [32768, 6144], P('dp', 'mp'), may hold values from -0.1875 to 0.1875
- hidden: bfloat16 [12288, 32768], P('mp', 'dp'), may hold values from -6 to 6
- feedback: float32 [12288, 6144], P('dp', 'mp'), may hold values from -6 to 6
- momentum: float32 [12288, 6144], P('dp', 'mp'), may hold values from -4 to 4
- q_start: float32 [12288, 8], replicated, may hold values from -6 to 6
Outputs:
- new_feedback: float32 [12288, 6144], P('dp', 'mp')
- new_momentum: float32 [12288, 6144], P('dp', 'mp')
- q_next: float32 [12288, 8], replicated
The draws below stay inside these ranges and needn't reach their ends.
All inputs are finite; a program needn't handle non-finite values.
Results may differ from the reference program's by a relative error of at most 0.0003.
Values may be sent and summed in bfloat16 or wider, within the bound.
No kernel may reach another device: no remote copies, remote signals or barrier semaphores. Data moves between devices by JAX's collectives and lax.ppermute only.
A program may use at most 64 MiB of HBM per device.

```python
import jax
import jax.numpy as jnp
from jax import lax

D = 6144
COLS = 12288
RANK = 8
TOK = 1024
TOKENS = 32768
N_DP = 32


def shard_levels(rng, dims, shards, least, high):
    loudness = 1.0
    for axis_at, blocks in shards:
        heights = jax.random.uniform(jax.random.fold_in(jax.random.fold_in(rng, 6), axis_at), (blocks,), jnp.float32, least / len(shards), high / len(shards))
        loudness = loudness * jnp.repeat(jnp.exp(heights), dims[axis_at] // blocks).reshape((-1,) + (1,) * (len(dims) - 1 - axis_at))
    return loudness


def noise(own_key, extent, spread, reach, pieces=(), held_as=jnp.bfloat16):
    array = spread * jax.random.normal(own_key, extent, jnp.float32)
    if pieces:
        array = array * shard_levels(own_key, extent, pieces, -0.22, 0.18)
    return jnp.clip(array, -reach, reach).astype(held_as)


def setup_inputs(seed: int = 0) -> dict:
    arg_keys = jax.random.split(jax.random.key(seed), 6)
    return {
        "activations": noise(arg_keys[0], (TOKENS, D), TOK ** -0.5, 0.1875, ((0, 32), (1, 16))),
        "hidden": noise(arg_keys[1], (COLS, TOKENS), 1.0, 6.0, ((0, 16), (1, 32))),
        "feedback": noise(arg_keys[2], (COLS, D), 1.0, 6.0, ((0, 32), (1, 16)), jnp.float32),
        "momentum": noise(arg_keys[3], (COLS, D), 0.3, 4.0, ((0, 32), (1, 16)), jnp.float32),
        "q_start": noise(arg_keys[4], (COLS, RANK), 1.0, 6.0, (), jnp.float32),
    }


decay_rate = 0.9

def reference(activations, hidden, feedback, momentum, q_start):
    high = lax.Precision.HIGHEST
    own = COLS // N_DP
    act_split = activations.reshape(N_DP, TOK, D).astype(jnp.float32)
    hid_split = jnp.transpose(hidden.reshape(COLS, N_DP, TOK), (1, 0, 2))
    errors = feedback.astype(jnp.float32)

    def token_side(hid_rows):
        return jnp.einsum('ct,cr->tr', hid_rows.astype(jnp.float32), q_start, precision=high)
    token_q = lax.map(token_side, hid_split)
    p_sum = jnp.einsum('ntd,ntr->dr', act_split, token_q, precision=high)
    p_sum = p_sum + jnp.einsum('cd,cr->dr', errors, q_start, precision=high)
    gram_mat = jnp.einsum('dr,ds->rs', p_sum, p_sum, precision=high)
    factor = jnp.linalg.cholesky(gram_mat)
    ortho = lax.linalg.triangular_solve(factor, p_sum, left_side=False, lower=True, transpose_a=True)
    token_o = jnp.einsum('ntd,dr->ntr', act_split, ortho, precision=high)

    def hidden_side(pair):
        hid_rows, factors = pair
        return jnp.einsum('ct,tr->cr', hid_rows.astype(jnp.float32), factors, precision=high)
    q_terms = jnp.sum(lax.map(hidden_side, (hid_split, token_o)), axis=0)
    q_next = (q_terms + jnp.dot(errors, ortho, precision=high)) / N_DP
    approx = jnp.einsum('cr,dr->cd', q_next, ortho, precision=high)
    blocks = hidden.reshape(N_DP, own, N_DP, TOK)
    index = jnp.arange(N_DP)
    own_hidden = blocks[index, :, index, :].astype(jnp.float32)
    own_grad = jnp.einsum('nct,ntd->ncd', own_hidden, act_split, precision=high).reshape(COLS, D)
    new_feedback = own_grad + errors - approx
    new_momentum = decay_rate * momentum + approx
    return (new_feedback, new_momentum, q_next)
```

```python
import jax
import jax.numpy as jnp
from jax import lax
from jax.sharding import Mesh, PartitionSpec as P

decay_rate = 0.9
high = lax.Precision.HIGHEST


def split_parts(x):
    a = lax.reduce_precision(x, 8, 7)
    r = x - a
    b = lax.reduce_precision(r, 8, 7)
    c = r - b
    return jnp.concatenate([a, b, c], 0).astype(jnp.bfloat16)


def thin_dot(x, wide, dims):
    y = lax.dot_general(
        split_parts(x), wide, (dims, ((), ())), preferred_element_type=jnp.float32
    )
    r = x.shape[0]
    return (y[2 * r :] + y[r : 2 * r]) + y[:r]


def copies(x, axes, count):
    return lax.all_to_all(jnp.broadcast_to(x[None], (count,) + x.shape), axes, 0, 0)


def per_device(activations, hidden, feedback, momentum, q_start):
    nz, nc, nx, ny = (lax.axis_size(a) for a in ("z", "c", "x", "y"))
    plane = ("x", "y")
    n_dp, n_mp = nz * nc, nx * ny
    z, core = lax.axis_index("z"), lax.axis_index("c")
    replica = z * nc + core
    shard = lax.axis_index("x") * ny + lax.axis_index("y")
    rank = q_start.shape[1]
    cols_mp, toks = hidden.shape
    cols_dp = feedback.shape[0]
    width = activations.shape[1]
    own_start = replica * cols_dp
    root_dev = own_start // cols_mp
    piece = lax.dynamic_slice_in_dim(hidden, own_start % cols_mp, cols_dp, 0)
    piece = jnp.where(shard == root_dev, piece, jnp.zeros_like(piece))
    own_hidden = lax.psum(piece, plane)

    q_rows = q_start.T
    q_block = lax.dynamic_slice_in_dim(q_rows, shard * cols_mp, cols_mp, 1)
    q_owned = lax.dynamic_slice_in_dim(q_rows, own_start, cols_dp, 1)
    token_part = thin_dot(q_block, hidden, ((1,), (0,)))
    token_q = copies(token_part, plane, n_mp).sum(0)
    p_err = jnp.dot(q_owned, feedback, precision=high)
    p_part = thin_dot(token_q, activations, ((1,), (0,))) + p_err
    p_pair = lax.all_gather(p_part, "c").sum(0)
    p_sum = copies(p_pair, "z", nz).sum(0)

    u_part = thin_dot(p_sum, activations, ((1,), (1,)))
    err_part = lax.dot_general(
        p_sum, feedback, (((1,), (1,)), ((), ())), precision=high
    )
    gram_part = lax.dot_general(p_sum, p_sum, (((1,), (1,)), ((), ())), precision=high)
    packed = jnp.concatenate(
        [u_part, err_part, jnp.pad(gram_part, ((0, 0), (0, 128 - rank)))], 1
    )
    packed = copies(packed, plane, n_mp).sum(0)
    u = packed[:, :toks]
    err = packed[:, toks : toks + cols_dp]
    gram_mat = packed[:, toks + cols_dp : toks + cols_dp + rank]
    factor = jnp.linalg.cholesky(gram_mat)
    inverse = lax.linalg.triangular_solve(
        factor, jnp.eye(rank, dtype=jnp.float32), left_side=True, lower=True
    )
    hid = thin_dot(u, hidden, ((1,), (1,)))
    hid = hid.reshape(rank, nc, cols_mp // nc)
    mine = (shard == root_dev) & (jnp.arange(nc) == core)
    hid = hid + jnp.where(mine[None, :, None], err[:, None, :], 0.0)
    hid = hid.reshape(rank, cols_mp)
    half = lax.all_gather(hid, "c").sum(0)
    half = lax.dynamic_slice_in_dim(half, core * cols_dp, cols_dp, 1)
    half = copies(half, "z", nz).sum(0)
    block = jnp.dot(inverse, half, precision=high) / n_dp
    blocks = copies(block, ("x", "y", "c"), n_dp)
    q_next = jnp.transpose(blocks, (1, 0, 2)).reshape(rank, -1).T
    q_mine = lax.dynamic_index_in_dim(blocks, replica, 0, keepdims=False)
    ortho = jnp.dot(inverse, p_sum, precision=high)
    approx = lax.dot_general(q_mine, ortho, (((0,), (0,)), ((), ())), precision=high)
    own_grad = jnp.dot(own_hidden, activations, preferred_element_type=jnp.float32)
    new_feedback = own_grad + feedback - approx
    new_momentum = decay_rate * momentum + approx
    return (new_feedback, new_momentum, q_next)


def solution(mesh):
    grid = Mesh(mesh.devices.reshape(16, 2, 4, 4), ("z", "c", "x", "y"))
    dp, mp = ("z", "c"), ("x", "y")
    placed = (P(dp, mp), P(mp, dp), P(dp, mp), P(dp, mp), P())
    return jax.shard_map(
        per_device,
        mesh=grid,
        in_specs=placed,
        out_specs=(P(dp, mp), P(dp, mp), P()),
        check_vma=False,
    )
```

```python
import jax
import jax.numpy as jnp
import numpy as np
from jax import lax
from jax.sharding import Mesh, PartitionSpec as P

decay_rate = 0.9
high = lax.Precision.HIGHEST


def split_parts(x):
    a = lax.reduce_precision(x, 8, 7)
    r = x - a
    b = lax.reduce_precision(r, 8, 7)
    c = r - b
    return jnp.concatenate([a, b, c], 0).astype(jnp.bfloat16)


def thin_dot(x, wide, dims):
    y = lax.dot_general(
        split_parts(x), wide, (dims, ((), ())), preferred_element_type=jnp.float32
    )
    r = x.shape[0]
    return (y[2 * r :] + y[r : 2 * r]) + y[:r]


def copies(x, axes, count):
    return lax.all_to_all(jnp.broadcast_to(x[None], (count,) + x.shape), axes, 0, 0)


def tie(x, after):
    return lax.optimization_barrier((x, after))[0]


def tree_rounds(nz, nc, nx, ny):
    def device(z, c, x, y):
        return ((z * nc + c) * nx + x) * ny + y

    rounds = []
    known = {c: [(0, 0)] for c in range(nc)}
    steps = ((nx // 2, 0), (0, ny // 2), (nx // 4, 0), (0, ny // 4))
    for step in steps:
        pairs = []
        for c in range(nc):
            dx, dy = step if c == 0 else (step[1], step[0])
            fresh = [((a + dx) % nx, (b + dy) % ny) for a, b in known[c]]
            for z in range(nz):
                ox, oy = z // ny, z % ny
                for (a, b), (e, f) in zip(known[c], fresh):
                    source = device(z, c, (ox + a) % nx, (oy + b) % ny)
                    target = device(z, c, (ox + e) % nx, (oy + f) % ny)
                    pairs.append((source, target))
            known[c] = known[c] + fresh
        rounds.append(pairs)
    return rounds


def per_device(activations, hidden, feedback, momentum, q_start):
    nz, nc, nx, ny = (lax.axis_size(a) for a in ("z", "c", "x", "y"))
    plane = ("x", "y")
    n_dp, n_mp = nz * nc, nx * ny
    z, core = lax.axis_index("z"), lax.axis_index("c")
    replica = z * nc + core
    shard = lax.axis_index("x") * ny + lax.axis_index("y")
    rank = q_start.shape[1]
    cols_mp, toks = hidden.shape
    cols_dp = feedback.shape[0]
    width = activations.shape[1]
    own_start = replica * cols_dp
    root_dev = own_start // cols_mp
    rounds = tree_rounds(nz, nc, nx, ny)
    me = lax.axis_index(("z", "c", "x", "y"))

    def send(held, k):
        got = lax.ppermute(held, ("z", "c", "x", "y"), rounds[k])
        takers = np.zeros(nz * nc * nx * ny, np.bool_)
        takers[[t for _, t in rounds[k]]] = True
        return got, jnp.asarray(takers)[me]

    q_rows = q_start.T
    q_block = lax.dynamic_slice_in_dim(q_rows, shard * cols_mp, cols_mp, 1)
    q_owned = lax.dynamic_slice_in_dim(q_rows, own_start, cols_dp, 1)
    token_part = thin_dot(q_block, hidden, ((1,), (0,)))
    hid_late = tie(hidden, token_part)
    held = lax.dynamic_slice_in_dim(hid_late, core * cols_dp, cols_dp, 0)
    got, takes = send(held, 0)
    token_q = copies(token_part, plane, n_mp).sum(0)
    p_err = jnp.dot(q_owned, feedback, precision=high)
    p_part = thin_dot(token_q, activations, ((1,), (0,))) + p_err
    p_pair = lax.all_gather(p_part, "c").sum(0)
    held = jnp.where(takes, tie(got, p_pair), held)
    got, takes = send(held, 1)
    p_sum = copies(p_pair, "z", nz).sum(0)

    u_part = thin_dot(p_sum, activations, ((1,), (1,)))
    err_part = lax.dot_general(
        p_sum, feedback, (((1,), (1,)), ((), ())), precision=high
    )
    gram_part = lax.dot_general(p_sum, p_sum, (((1,), (1,)), ((), ())), precision=high)
    packed = jnp.concatenate(
        [u_part, err_part, jnp.pad(gram_part, ((0, 0), (0, 128 - rank)))], 1
    )
    held = jnp.where(takes, tie(got, packed), held)
    got, takes = send(held, 2)
    packed = copies(packed, plane, n_mp).sum(0)
    u = packed[:, :toks]
    err = packed[:, toks : toks + cols_dp]
    gram_mat = packed[:, toks + cols_dp : toks + cols_dp + rank]
    factor = jnp.linalg.cholesky(gram_mat)
    inverse = lax.linalg.triangular_solve(
        factor, jnp.eye(rank, dtype=jnp.float32), left_side=True, lower=True
    )
    hid = thin_dot(u, hidden, ((1,), (1,)))
    hid = hid.reshape(rank, nc, cols_mp // nc)
    mine = (shard == root_dev) & (jnp.arange(nc) == core)
    hid = hid + jnp.where(mine[None, :, None], err[:, None, :], 0.0)
    hid = hid.reshape(rank, cols_mp)
    half = lax.all_gather(hid, "c").sum(0)
    half = lax.dynamic_slice_in_dim(half, core * cols_dp, cols_dp, 1)
    held = jnp.where(takes, tie(got, half), held)
    got, takes = send(held, 3)
    half = copies(half, "z", nz).sum(0)
    block = jnp.dot(inverse, half, precision=high) / n_dp
    held = jnp.where(takes, tie(got, block), held)
    own_grad = jnp.dot(held, activations, preferred_element_type=jnp.float32)
    base = own_grad + feedback
    blocks = copies(block, ("x", "y", "c"), n_dp)
    q_next = jnp.transpose(blocks, (1, 0, 2)).reshape(rank, -1).T
    q_mine = lax.dynamic_index_in_dim(blocks, replica, 0, keepdims=False)
    ortho = jnp.dot(inverse, p_sum, precision=high)
    approx = lax.dot_general(q_mine, ortho, (((0,), (0,)), ((), ())), precision=high)
    new_feedback = base - approx
    new_momentum = decay_rate * momentum + approx
    return (new_feedback, new_momentum, q_next)


def solution(mesh):
    grid = Mesh(mesh.devices.reshape(16, 2, 4, 4), ("z", "c", "x", "y"))
    dp, mp = ("z", "c"), ("x", "y")
    placed = (P(dp, mp), P(mp, dp), P(dp, mp), P(dp, mp), P())
    return jax.shard_map(
        per_device,
        mesh=grid,
        in_specs=placed,
        out_specs=(P(dp, mp), P(dp, mp), P()),
        check_vma=False,
    )
```

```python
import jax
import jax.numpy as jnp
from jax import lax
from jax.sharding import Mesh, PartitionSpec as P

decay_rate = 0.9
high = lax.Precision.HIGHEST


def split_parts(x):
    a = lax.reduce_precision(x, 8, 7)
    r = x - a
    b = lax.reduce_precision(r, 8, 7)
    c = r - b
    return jnp.concatenate([a, b, c], 0).astype(jnp.bfloat16)


def thin_dot(x, wide, dims):
    y = lax.dot_general(
        split_parts(x), wide, (dims, ((), ())), preferred_element_type=jnp.float32
    )
    r = x.shape[0]
    return (y[2 * r :] + y[r : 2 * r]) + y[:r]


def copies(x, axes, count):
    return lax.all_to_all(jnp.broadcast_to(x[None], (count,) + x.shape), axes, 0, 0)


def tie(x, after):
    return lax.optimization_barrier((x, after))[0]


def tree_rounds(nz, nc, nx, ny):
    def device(z, c, x, y):
        return ((z * nc + c) * nx + x) * ny + y

    rounds = []
    known = {c: [(0, 0)] for c in range(nc)}
    steps = ((nx // 2, 0), (0, ny // 2), (nx // 4, 0), (0, ny // 4))
    for step in steps:
        pairs = []
        for c in range(nc):
            dx, dy = step if c == 0 else (step[1], step[0])
            fresh = [((a + dx) % nx, (b + dy) % ny) for a, b in known[c]]
            for z in range(nz):
                ox, oy = z // ny, z % ny
                for (a, b), (e, f) in zip(known[c], fresh):
                    source = device(z, c, (ox + a) % nx, (oy + b) % ny)
                    target = device(z, c, (ox + e) % nx, (oy + f) % ny)
                    pairs.append((source, target))
            known[c] = known[c] + fresh
        rounds.append(pairs)
    return rounds


def per_device(activations, hidden, feedback, momentum, q_start):
    nz, nc, nx, ny = (lax.axis_size(a) for a in ("z", "c", "x", "y"))
    plane = ("x", "y")
    n_dp, n_mp = nz * nc, nx * ny
    z, core = lax.axis_index("z"), lax.axis_index("c")
    replica = z * nc + core
    shard = lax.axis_index("x") * ny + lax.axis_index("y")
    rank = q_start.shape[1]
    cols_mp, toks = hidden.shape
    cols_dp = feedback.shape[0]
    width = activations.shape[1]
    own_start = replica * cols_dp
    root_dev = own_start // cols_mp
    rounds = tree_rounds(nz, nc, nx, ny)
    off_x = (lax.axis_index("x") - z // ny) % nx
    off_y = (lax.axis_index("y") - z % ny) % ny
    first = jnp.where(core == 0, off_x, off_y)
    second = jnp.where(core == 0, off_y, off_x)
    turn = jnp.where(first >= 2, 0, -1)
    turn = jnp.where(second >= 2, 1, turn)
    turn = jnp.where(first % 2 == 1, 2, turn)
    turn = jnp.where(second % 2 == 1, 3, turn)

    def send(held, k):
        return lax.ppermute(held, ("z", "c", "x", "y"), rounds[k])

    def take(held, got, k):
        return jnp.where(turn == k, got, held)

    q_rows = q_start.T
    q_block = lax.dynamic_slice_in_dim(q_rows, shard * cols_mp, cols_mp, 1)
    q_owned = lax.dynamic_slice_in_dim(q_rows, own_start, cols_dp, 1)
    token_part = thin_dot(q_block, hidden, ((1,), (0,)))
    hid_late = tie(hidden, token_part)
    held = lax.dynamic_slice_in_dim(hid_late, core * cols_dp, cols_dp, 0)
    got = send(held, 0)
    token_q = copies(token_part, plane, n_mp).sum(0)
    p_err = jnp.dot(q_owned, feedback, precision=high)
    p_part = thin_dot(token_q, activations, ((1,), (0,))) + p_err
    p_pair = lax.all_gather(p_part, "c").sum(0)
    held = take(held, tie(got, p_pair), 0)
    got = send(held, 1)
    part = rank // nc
    p_pair = lax.dynamic_slice_in_dim(p_pair, core * part, part, 0)
    p_half = copies(p_pair, "z", nz).sum(0)
    held = take(held, got, 1)
    got = send(held, 2)
    p_sum = lax.all_gather(p_half, "c", tiled=True)

    u_part = thin_dot(p_sum, activations, ((1,), (1,)))
    err_part = lax.dot_general(
        p_sum, feedback, (((1,), (1,)), ((), ())), precision=high
    )
    gram_part = lax.dot_general(p_sum, p_sum, (((1,), (1,)), ((), ())), precision=high)
    packed = jnp.concatenate(
        [u_part, err_part, jnp.pad(gram_part, ((0, 0), (0, 128 - rank)))], 1
    )
    packed = copies(packed, plane, n_mp).sum(0)
    u = packed[:, :toks]
    err = packed[:, toks : toks + cols_dp]
    gram_mat = packed[:, toks + cols_dp : toks + cols_dp + rank]
    factor = jnp.linalg.cholesky(gram_mat)
    inverse = lax.linalg.triangular_solve(
        factor, jnp.eye(rank, dtype=jnp.float32), left_side=True, lower=True
    )
    hid = thin_dot(u, hidden, ((1,), (1,)))
    hid = hid.reshape(rank, nc, cols_mp // nc)
    mine = (shard == root_dev) & (jnp.arange(nc) == core)
    hid = hid + jnp.where(mine[None, :, None], err[:, None, :], 0.0)
    hid = hid.reshape(rank, cols_mp)
    half = lax.all_gather(hid, "c").sum(0)
    half = lax.dynamic_slice_in_dim(half, core * cols_dp, cols_dp, 1)
    held = take(held, tie(got, half), 2)
    got = send(held, 3)
    half = copies(half, "z", nz).sum(0)
    block = jnp.dot(inverse, half, precision=high) / n_dp
    held = take(held, tie(got, block), 3)
    own_grad = jnp.dot(held, activations, preferred_element_type=jnp.float32)
    base = lax.optimization_barrier(own_grad + feedback)
    blocks = copies(block, ("x", "y", "c"), n_dp)
    q_next = jnp.transpose(blocks, (1, 0, 2)).reshape(rank, -1).T
    q_mine = lax.dynamic_index_in_dim(blocks, replica, 0, keepdims=False)
    ortho = jnp.dot(inverse, p_sum, precision=high)
    approx = lax.dot_general(q_mine, ortho, (((0,), (0,)), ((), ())), precision=high)
    new_feedback = base - approx
    new_momentum = decay_rate * momentum + approx
    return (new_feedback, new_momentum, q_next)


def solution(mesh):
    grid = Mesh(mesh.devices.reshape(16, 2, 4, 4), ("z", "c", "x", "y"))
    dp, mp = ("z", "c"), ("x", "y")
    placed = (P(dp, mp), P(mp, dp), P(dp, mp), P(dp, mp), P())
    return jax.shard_map(
        per_device,
        mesh=grid,
        in_specs=placed,
        out_specs=(P(dp, mp), P(dp, mp), P()),
        check_vma=False,
    )
```

```python
import jax
import jax.numpy as jnp
from jax import lax
from jax.experimental import pallas as pl
from jax.experimental.pallas import tpu as pltpu
from jax.sharding import Mesh, PartitionSpec as P

decay_rate = 0.9
high = lax.Precision.HIGHEST


def split_parts(x):
    a = lax.reduce_precision(x, 8, 7)
    r = x - a
    b = lax.reduce_precision(r, 8, 7)
    c = r - b
    return jnp.concatenate([a, b, c], 0).astype(jnp.bfloat16)


def thin_dot(x, wide, dims):
    y = lax.dot_general(
        split_parts(x), wide, (dims, ((), ())), preferred_element_type=jnp.float32
    )
    r = x.shape[0]
    return (y[2 * r :] + y[r : 2 * r]) + y[:r]


def copies(x, axes, count):
    return lax.all_to_all(jnp.broadcast_to(x[None], (count,) + x.shape), axes, 0, 0)


def near(x):
    return pltpu.with_memory_space_constraint(x, pltpu.VMEM)


def local(kernel, outs, micros, *args):
    whole = pl.BlockSpec(memory_space=pltpu.VMEM)
    size = sum(a.size * a.dtype.itemsize for a in args)
    return pl.pallas_call(
        kernel,
        out_shape=outs,
        in_specs=[whole] * len(args),
        out_specs=[whole] * len(outs),
        cost_estimate=pl.CostEstimate(
            flops=int(micros * 1e9), bytes_accessed=size, transcendentals=0
        ),
    )(*args)


def exact_dot(x, wide, dims):
    a = x.astype(jnp.bfloat16).astype(jnp.float32)
    r = x - a
    b = r.astype(jnp.bfloat16).astype(jnp.float32)
    parts = jnp.concatenate([a, b, r - b, jnp.zeros_like(x)], 0)
    y = lax.dot_general(
        parts.astype(jnp.bfloat16),
        wide,
        (dims, ((), ())),
        preferred_element_type=jnp.float32,
    )
    n = x.shape[0]
    return (y[2 * n : 3 * n] + y[n : 2 * n]) + y[:n]


def total(ref, lanes):
    y = ref[0, :, lanes]
    for i in range(1, ref.shape[0]):
        y = y + ref[i, :, lanes]
    return y


def early_kernel(hid, q, feed, err, piece):
    rows = feed.shape[0]
    core = lax.axis_index("c")
    replica = lax.axis_index("z") * lax.axis_size("c") + core
    own = q[:, pl.ds(pl.multiple_of(replica * rows, rows), rows)]
    err[...] = jnp.dot(
        own, feed[...], precision=high, preferred_element_type=jnp.float32
    )
    piece[...] = hid[pl.ds(pl.multiple_of(core * rows, rows), rows), :]


def left_kernel(got, act, err, out):
    tokens = total(got, slice(None))
    out[...] = exact_dot(tokens, act[...], ((1,), (0,))) + err[...]


def right_kernel(p_ref, act, feed, out):
    p = p_ref[...]
    rank, toks = p.shape[0], act.shape[0]
    rows = feed.shape[0]
    u = exact_dot(p, act[...], ((1,), (1,)))
    across = (((1,), (1,)), ((), ()))
    err = lax.dot_general(
        p, feed[...], across, precision=high, preferred_element_type=jnp.float32
    )
    square = jnp.concatenate([p, jnp.zeros((128 - rank, p.shape[1]), p.dtype)], 0)
    gram = lax.dot_general(
        p, square, across, precision=high, preferred_element_type=jnp.float32
    )
    for i in range(out.shape[0]):
        out[i, :, :toks] = u
        out[i, :, toks : toks + rows] = err
        out[i, :, toks + rows :] = gram


def hidden_kernel(got, hid, out, gram):
    toks, rows = hid.shape[1], out.shape[1] // 2
    u = total(got, slice(0, toks))
    err = total(got, slice(toks, toks + rows))
    gram[...] = total(got, slice(toks + rows, None))
    y = exact_dot(u, hid[...], ((1,), (1,)))
    shard = lax.axis_index("x") * lax.axis_size("y") + lax.axis_index("y")
    mine = jnp.where(shard == lax.axis_index("z"), 1.0, 0.0)
    upper = jnp.where(lax.axis_index("c") == 0, mine, 0.0)
    lower = mine - upper
    out[:, :rows] = y[:, :rows] + err * upper
    out[:, rows:] = y[:, rows:] + err * lower


def block_kernel(got, inverse, out):
    rows = total(got, slice(None))
    block = jnp.dot(
        inverse[...], rows, precision=high, preferred_element_type=jnp.float32
    )
    block = block * (1.0 / out.shape[0])
    for i in range(out.shape[0]):
        out[i] = block


def last_kernel(blocks, ortho, base, momentum, feed_out, mom_out, q_out):
    count, _, rows = blocks.shape
    replica = lax.axis_index("z") * lax.axis_size("c") + lax.axis_index("c")
    mine = blocks[replica]
    approx = lax.dot_general(
        mine,
        ortho[...],
        (((0,), (0,)), ((), ())),
        precision=high,
        preferred_element_type=jnp.float32,
    )
    feed_out[...] = base[...] - approx
    mom_out[...] = decay_rate * momentum[...] + approx
    for i in range(count):
        q_out[:, i * rows : (i + 1) * rows] = blocks[i]


def tie(x, after):
    return lax.optimization_barrier((x, after))[0]


def tree_rounds(nz, nc, nx, ny):
    def device(z, c, x, y):
        return ((z * nc + c) * nx + x) * ny + y

    rounds = []
    known = {c: [(0, 0)] for c in range(nc)}
    steps = ((nx // 2, 0), (0, ny // 2), (nx // 4, 0), (0, ny // 4))
    for step in steps:
        pairs = []
        for c in range(nc):
            dx, dy = step if c == 0 else (step[1], step[0])
            fresh = [((a + dx) % nx, (b + dy) % ny) for a, b in known[c]]
            for z in range(nz):
                ox, oy = z // ny, z % ny
                for (a, b), (e, f) in zip(known[c], fresh):
                    source = device(z, c, (ox + a) % nx, (oy + b) % ny)
                    target = device(z, c, (ox + e) % nx, (oy + f) % ny)
                    pairs.append((source, target))
            known[c] = known[c] + fresh
        rounds.append(pairs)
    return rounds


def per_device(activations, hidden, feedback, momentum, q_start):
    nz, nc, nx, ny = (lax.axis_size(a) for a in ("z", "c", "x", "y"))
    plane = ("x", "y")
    n_dp, n_mp = nz * nc, nx * ny
    z, core = lax.axis_index("z"), lax.axis_index("c")
    replica = z * nc + core
    shard = lax.axis_index("x") * ny + lax.axis_index("y")
    rank = q_start.shape[1]
    cols_mp, toks = hidden.shape
    cols_dp = feedback.shape[0]
    width = activations.shape[1]
    own_start = replica * cols_dp
    root_dev = own_start // cols_mp
    rounds = tree_rounds(nz, nc, nx, ny)
    off_x = (lax.axis_index("x") - z // ny) % nx
    off_y = (lax.axis_index("y") - z % ny) % ny
    first = jnp.where(core == 0, off_x, off_y)
    second = jnp.where(core == 0, off_y, off_x)
    turn = jnp.where(first >= 2, 0, -1)
    turn = jnp.where(second >= 2, 1, turn)
    turn = jnp.where(first % 2 == 1, 2, turn)
    turn = jnp.where(second % 2 == 1, 3, turn)

    def send(held, k):
        return lax.ppermute(held, ("z", "c", "x", "y"), rounds[k])

    def take(held, got, k):
        return jnp.where(turn == k, got, held)

    q_rows = q_start.T
    q_block = lax.dynamic_slice_in_dim(q_rows, shard * cols_mp, cols_mp, 1)
    token_part = thin_dot(q_block, hidden, ((1,), (0,)))
    f32 = jnp.float32
    act_near, hid_near, feed_near = near(activations), near(hidden), near(feedback)
    p_err, held = local(
        early_kernel,
        [
            pltpu.VMEM((rank, width), f32),
            pltpu.VMEM((cols_dp, toks), hidden.dtype),
        ],
        1.5,
        tie(hid_near, token_part),
        near(q_rows),
        feed_near,
    )
    got = send(held, 0)
    tokens = near(copies(token_part, plane, n_mp))
    (p_part,) = local(
        left_kernel,
        [pltpu.VMEM((rank, width), f32)],
        1,
        tokens,
        act_near,
        p_err,
    )
    p_pair = lax.all_gather(p_part, "c").sum(0)
    held = take(held, tie(got, p_pair), 0)
    got = send(held, 1)
    part = rank // nc
    p_pair = lax.dynamic_slice_in_dim(p_pair, core * part, part, 0)
    p_half = copies(p_pair, "z", nz).sum(0)
    held = take(held, got, 1)
    got = send(held, 2)
    p_sum = lax.all_gather(p_half, "c", tiled=True)

    (packed,) = local(
        right_kernel,
        [pltpu.VMEM((n_mp, rank, toks + cols_dp + 128), f32)],
        2,
        near(p_sum),
        act_near,
        feed_near,
    )
    packed = near(lax.all_to_all(packed, plane, 0, 0))
    hid, gram_mat = local(
        hidden_kernel,
        [pltpu.VMEM((rank, cols_mp), f32), pltpu.VMEM((rank, 128), f32)],
        1,
        packed,
        hid_near,
    )
    gram_mat = gram_mat[:, :rank]
    factor = jnp.linalg.cholesky(gram_mat)
    inverse = lax.linalg.triangular_solve(
        factor, jnp.eye(rank, dtype=jnp.float32), left_side=True, lower=True
    )
    half = lax.all_gather(hid, "c").sum(0)
    half = lax.dynamic_slice_in_dim(half, core * cols_dp, cols_dp, 1)
    held = take(held, tie(got, half), 2)
    got = send(held, 3)
    half = near(copies(half, "z", nz))
    (block,) = local(
        block_kernel,
        [pltpu.VMEM((n_dp, rank, cols_dp), f32)],
        1,
        half,
        near(inverse),
    )
    held = take(held, tie(got, block), 3)
    own_grad = jnp.dot(held, activations, preferred_element_type=jnp.float32)
    base = lax.optimization_barrier(own_grad + feedback)
    blocks = near(lax.all_to_all(block, ("x", "y", "c"), 0, 0))
    ortho = jnp.dot(inverse, p_sum, precision=high)
    new_feedback, new_momentum, q_next = local(
        last_kernel,
        [
            jax.ShapeDtypeStruct(feedback.shape, f32),
            jax.ShapeDtypeStruct(momentum.shape, f32),
            jax.ShapeDtypeStruct(q_rows.shape, f32),
        ],
        2,
        blocks,
        near(ortho),
        near(base),
        near(momentum),
    )
    return (new_feedback, new_momentum, q_next.T)


def solution(mesh):
    grid = Mesh(mesh.devices.reshape(16, 2, 4, 4), ("z", "c", "x", "y"))
    dp, mp = ("z", "c"), ("x", "y")
    placed = (P(dp, mp), P(mp, dp), P(dp, mp), P(dp, mp), P())
    return jax.shard_map(
        per_device,
        mesh=grid,
        in_specs=placed,
        out_specs=(P(dp, mp), P(dp, mp), P()),
        check_vma=False,
    )
```

```python
import jax
import jax.numpy as jnp
from jax import lax
from jax.experimental import pallas as pl
from jax.experimental.pallas import tpu as pltpu
from jax.sharding import Mesh, PartitionSpec as P

decay_rate = 0.9
high = lax.Precision.HIGHEST


def split_parts(x):
    a = lax.reduce_precision(x, 8, 7)
    r = x - a
    b = lax.reduce_precision(r, 8, 7)
    c = r - b
    return jnp.concatenate([a, b, c], 0).astype(jnp.bfloat16)


def thin_dot(x, wide, dims):
    y = lax.dot_general(
        split_parts(x), wide, (dims, ((), ())), preferred_element_type=jnp.float32
    )
    r = x.shape[0]
    return (y[2 * r :] + y[r : 2 * r]) + y[:r]


def copies(x, axes, count):
    return lax.all_to_all(jnp.broadcast_to(x[None], (count,) + x.shape), axes, 0, 0)


def near(x):
    return pltpu.with_memory_space_constraint(x, pltpu.VMEM)


def local(kernel, outs, micros, *args):
    whole = pl.BlockSpec(memory_space=pltpu.VMEM)
    size = sum(a.size * a.dtype.itemsize for a in args)
    return pl.pallas_call(
        kernel,
        out_shape=outs,
        in_specs=[whole] * len(args),
        out_specs=[whole] * len(outs),
        compiler_params=pltpu.CompilerParams(vmem_limit_bytes=8 * 2**20),
        cost_estimate=pl.CostEstimate(
            flops=int(micros * 1e9), bytes_accessed=size, transcendentals=0
        ),
    )(*args)


def exact_dot(x, wide, dims):
    a = x.astype(jnp.bfloat16).astype(jnp.float32)
    r = x - a
    b = r.astype(jnp.bfloat16).astype(jnp.float32)
    parts = jnp.concatenate([a, b, r - b, jnp.zeros_like(x)], 0)
    y = lax.dot_general(
        parts.astype(jnp.bfloat16),
        wide,
        (dims, ((), ())),
        preferred_element_type=jnp.float32,
    )
    n = x.shape[0]
    return (y[2 * n : 3 * n] + y[n : 2 * n]) + y[:n]


def total(ref, lanes):
    y = ref[0, :, lanes]
    for i in range(1, ref.shape[0]):
        y = y + ref[i, :, lanes]
    return y


def early_kernel(q, feed, act, err, act_out):
    err[...] = jnp.dot(
        q[...], feed[...], precision=high, preferred_element_type=jnp.float32
    )
    act_out[...] = act[...]


def left_kernel(got, act, err, out):
    tokens = total(got, slice(None))
    out[...] = exact_dot(tokens, act[...], ((1,), (0,))) + err[...]


def right_kernel(p_ref, act, feed, out):
    p = p_ref[...]
    rank, toks = p.shape[0], act.shape[0]
    rows = feed.shape[0]
    u = exact_dot(p, act[...], ((1,), (1,)))
    across = (((1,), (1,)), ((), ()))
    err = lax.dot_general(
        p, feed[...], across, precision=high, preferred_element_type=jnp.float32
    )
    square = jnp.concatenate([p, jnp.zeros((128 - rank, p.shape[1]), p.dtype)], 0)
    gram = lax.dot_general(
        p, square, across, precision=high, preferred_element_type=jnp.float32
    )
    for i in range(out.shape[0]):
        out[i, :, :toks] = u
        out[i, :, toks : toks + rows] = err
        out[i, :, toks + rows :] = gram


def hidden_kernel(got, hid, out, gram):
    toks, rows = hid.shape[1], out.shape[1] // 2
    u = total(got, slice(0, toks))
    err = total(got, slice(toks, toks + rows))
    gram[...] = total(got, slice(toks + rows, None))
    y = exact_dot(u, hid[...], ((1,), (1,)))
    shard = lax.axis_index("x") * lax.axis_size("y") + lax.axis_index("y")
    mine = jnp.where(shard == lax.axis_index("z"), 1.0, 0.0)
    upper = jnp.where(lax.axis_index("c") == 0, mine, 0.0)
    lower = mine - upper
    out[:, :rows] = y[:, :rows] + err * upper
    out[:, rows:] = y[:, rows:] + err * lower


def block_kernel(got, inverse, out):
    rows = total(got, slice(None))
    block = jnp.dot(
        inverse[...], rows, precision=high, preferred_element_type=jnp.float32
    )
    block = block * (1.0 / out.shape[0])
    for i in range(out.shape[0]):
        out[i] = block


def last_kernel(blocks, ortho, base, momentum, feed_out, mom_out, q_out):
    count, _, rows = blocks.shape
    replica = lax.axis_index("z") * lax.axis_size("c") + lax.axis_index("c")
    mine = blocks[replica]
    approx = lax.dot_general(
        mine,
        ortho[...],
        (((0,), (0,)), ((), ())),
        precision=high,
        preferred_element_type=jnp.float32,
    )
    feed_out[...] = base[...] - approx
    mom_out[...] = decay_rate * momentum[...] + approx
    for i in range(count):
        q_out[:, i * rows : (i + 1) * rows] = blocks[i]


def tie(x, after):
    return lax.optimization_barrier((x, after))[0]


def tree_rounds(nz, nc, nx, ny):
    def device(z, c, x, y):
        return ((z * nc + c) * nx + x) * ny + y

    rounds = []
    known = {c: [(0, 0)] for c in range(nc)}
    steps = ((nx // 2, 0), (0, ny // 2), (nx // 4, 0), (0, ny // 4))
    for step in steps:
        pairs = []
        for c in range(nc):
            dx, dy = step if c == 0 else (step[1], step[0])
            fresh = [((a + dx) % nx, (b + dy) % ny) for a, b in known[c]]
            for z in range(nz):
                ox, oy = z // ny, z % ny
                for (a, b), (e, f) in zip(known[c], fresh):
                    source = device(z, c, (ox + a) % nx, (oy + b) % ny)
                    target = device(z, c, (ox + e) % nx, (oy + f) % ny)
                    pairs.append((source, target))
            known[c] = known[c] + fresh
        rounds.append(pairs)
    return rounds


def per_device(activations, hidden, feedback, momentum, q_start):
    nz, nc, nx, ny = (lax.axis_size(a) for a in ("z", "c", "x", "y"))
    plane = ("x", "y")
    n_dp, n_mp = nz * nc, nx * ny
    z, core = lax.axis_index("z"), lax.axis_index("c")
    replica = z * nc + core
    shard = lax.axis_index("x") * ny + lax.axis_index("y")
    rank = q_start.shape[1]
    cols_mp, toks = hidden.shape
    cols_dp = feedback.shape[0]
    width = activations.shape[1]
    own_start = replica * cols_dp
    root_dev = own_start // cols_mp
    rounds = tree_rounds(nz, nc, nx, ny)
    off_x = (lax.axis_index("x") - z // ny) % nx
    off_y = (lax.axis_index("y") - z % ny) % ny
    first = jnp.where(core == 0, off_x, off_y)
    second = jnp.where(core == 0, off_y, off_x)
    turn = jnp.where(first >= 2, 0, -1)
    turn = jnp.where(second >= 2, 1, turn)
    turn = jnp.where(first % 2 == 1, 2, turn)
    turn = jnp.where(second % 2 == 1, 3, turn)

    def send(held, k):
        return lax.ppermute(held, ("z", "c", "x", "y"), rounds[k])

    def take(held, got, k):
        return jnp.where(turn == k, got, held)

    q_rows = q_start.T
    q_block = lax.dynamic_slice_in_dim(q_rows, shard * cols_mp, cols_mp, 1)
    token_part = thin_dot(q_block, hidden, ((1,), (0,)))
    f32 = jnp.float32
    act_near, hid_near, feed_near = near(activations), near(hidden), near(feedback)
    q_owned = lax.dynamic_slice_in_dim(q_rows, own_start, cols_dp, 1)
    p_err, act_near = local(
        early_kernel,
        [
            pltpu.VMEM((rank, width), f32),
            pltpu.VMEM(activations.shape, activations.dtype),
        ],
        1.5,
        near(q_owned),
        tie(feed_near, token_part),
        act_near,
    )
    hid_late = tie(hidden, p_err)
    held = lax.dynamic_slice_in_dim(hid_late, core * cols_dp, cols_dp, 0)
    got = send(held, 0)
    tokens = near(copies(token_part, plane, n_mp))
    (p_part,) = local(
        left_kernel,
        [pltpu.VMEM((rank, width), f32)],
        1,
        tokens,
        near(act_near),
        near(p_err),
    )
    p_pair = lax.all_gather(p_part, "c").sum(0)
    held = take(held, tie(got, p_pair), 0)
    got = send(held, 1)
    part = rank // nc
    p_pair = lax.dynamic_slice_in_dim(p_pair, core * part, part, 0)
    p_half = copies(p_pair, "z", nz).sum(0)
    held = take(held, got, 1)
    got = send(held, 2)
    p_sum = lax.all_gather(p_half, "c", tiled=True)

    (packed,) = local(
        right_kernel,
        [pltpu.VMEM((n_mp, rank, toks + cols_dp + 128), f32)],
        2,
        near(p_sum),
        near(act_near),
        feed_near,
    )
    packed = near(lax.all_to_all(packed, plane, 0, 0))
    hid, gram_mat = local(
        hidden_kernel,
        [pltpu.VMEM((rank, cols_mp), f32), pltpu.VMEM((rank, 128), f32)],
        1,
        packed,
        hid_near,
    )
    gram_mat = gram_mat[:, :rank]
    half = lax.all_gather(hid, "c").sum(0)
    half = lax.dynamic_slice_in_dim(half, core * cols_dp, cols_dp, 1)
    held = take(held, tie(got, half), 2)
    got = send(held, 3)
    gram_mat = tie(gram_mat, half)
    factor = jnp.linalg.cholesky(gram_mat)
    inverse = lax.linalg.triangular_solve(
        factor, jnp.eye(rank, dtype=jnp.float32), left_side=True, lower=True
    )
    half = near(copies(half, "z", nz))
    (block,) = local(
        block_kernel,
        [pltpu.VMEM((n_dp, rank, cols_dp), f32)],
        1,
        half,
        near(inverse),
    )
    held = take(held, tie(got, block), 3)
    own_grad = jnp.dot(held, act_near, preferred_element_type=jnp.float32)
    base = lax.optimization_barrier(own_grad + feedback)
    blocks = near(lax.all_to_all(block, ("x", "y", "c"), 0, 0))
    ortho = jnp.dot(inverse, p_sum, precision=high)
    new_feedback, new_momentum, q_next = local(
        last_kernel,
        [
            jax.ShapeDtypeStruct(feedback.shape, f32),
            jax.ShapeDtypeStruct(momentum.shape, f32),
            jax.ShapeDtypeStruct(q_rows.shape, f32),
        ],
        2,
        blocks,
        near(ortho),
        near(base),
        near(momentum),
    )
    return (new_feedback, new_momentum, q_next.T)


def solution(mesh):
    grid = Mesh(mesh.devices.reshape(16, 2, 4, 4), ("z", "c", "x", "y"))
    dp, mp = ("z", "c"), ("x", "y")
    placed = (P(dp, mp), P(mp, dp), P(dp, mp), P(dp, mp), P())
    return jax.shard_map(
        per_device,
        mesh=grid,
        in_specs=placed,
        out_specs=(P(dp, mp), P(dp, mp), P()),
        check_vma=False,
    )
```

```python
import jax
import jax.numpy as jnp
from jax import lax
from jax.experimental import pallas as pl
from jax.experimental.pallas import tpu as pltpu
from jax.sharding import Mesh, PartitionSpec as P

decay_rate = 0.9
high = lax.Precision.HIGHEST


def copies(x, axes, count):
    return lax.all_to_all(jnp.broadcast_to(x[None], (count,) + x.shape), axes, 0, 0)


def near(x):
    return pltpu.with_memory_space_constraint(x, pltpu.VMEM)


def local(kernel, outs, micros, *args):
    whole = pl.BlockSpec(memory_space=pltpu.VMEM)
    size = sum(a.size * a.dtype.itemsize for a in args)
    return pl.pallas_call(
        kernel,
        out_shape=outs,
        in_specs=[whole] * len(args),
        out_specs=[whole] * len(outs),
        compiler_params=pltpu.CompilerParams(vmem_limit_bytes=4 * 2**20),
        cost_estimate=pl.CostEstimate(
            flops=int(micros * 4e9), bytes_accessed=size, transcendentals=0
        ),
    )(*args)


def exact_dot(x, wide, dims):
    y = lax.dot_general(
        parts_of(x), wide, (dims, ((), ())), preferred_element_type=jnp.float32
    )
    n = x.shape[0]
    return (y[2 * n : 3 * n] + y[n : 2 * n]) + y[:n]


def total(ref, lanes):
    y = ref[0, :, lanes]
    for i in range(1, ref.shape[0]):
        y = y + ref[i, :, lanes]
    return y


def parts_of(x):
    a = x.astype(jnp.bfloat16).astype(jnp.float32)
    r = x - a
    b = r.astype(jnp.bfloat16).astype(jnp.float32)
    return jnp.concatenate([a, b, r - b, jnp.zeros_like(x)], 0).astype(jnp.bfloat16)


def start_kernel(q, hid, out, q_own, piece_out, q_near, held, row, sems, done):
    rows, own_rows = hid.shape[0], q_own.shape[1]
    count = sems.shape[0] - 2
    step = rows // count
    shard = lax.axis_index("x") * lax.axis_size("y") + lax.axis_index("y")
    replica = lax.axis_index("z") * lax.axis_size("c") + lax.axis_index("c")
    mine = q.at[:, pl.ds(pl.multiple_of(shard * rows, rows), rows)]
    own = q.at[:, pl.ds(pl.multiple_of(replica * own_rows, own_rows), own_rows)]
    first = pltpu.make_async_copy(mine, q_near, sems.at[count])
    last = pltpu.make_async_copy(own, q_own, sems.at[count + 1])
    loads = []
    for i in range(count):
        piece = pl.ds(i * step, step)
        loads.append(pltpu.make_async_copy(hid.at[piece], held.at[piece], sems.at[i]))
    for load in [first] + loads + [last]:
        load.start()
    first.wait()
    parts = parts_of(q_near[...])
    y = jnp.zeros((parts.shape[0], hid.shape[1]), jnp.float32)
    for i in range(count):
        loads[i].wait()
        y = y + jnp.dot(
            parts[:, i * step : (i + 1) * step],
            held[i * step : (i + 1) * step, :],
            preferred_element_type=jnp.float32,
        )
    n = row.shape[0]
    row[...] = (y[2 * n : 3 * n] + y[n : 2 * n]) + y[:n]
    sends = [
        pltpu.make_async_copy(row, out.at[i], done.at[i]) for i in range(out.shape[0])
    ]
    for send in sends:
        send.start()
    core = lax.axis_index("c")
    piece_out[...] = held[pl.ds(pl.multiple_of(core * own_rows, own_rows), own_rows), :]
    last.wait()
    for send in sends:
        send.wait()


def early_kernel(q, feed, err):
    err[...] = jnp.dot(
        q[...], feed[...], precision=high, preferred_element_type=jnp.float32
    )


def left_kernel(got, act, err, out):
    tokens = total(got, slice(None))
    out[...] = exact_dot(tokens, act[...], ((1,), (0,))) + err[...]


def right_kernel(p_ref, act, feed, out):
    p = p_ref[...]
    rank, toks = p.shape[0], act.shape[0]
    rows = feed.shape[0]
    u = exact_dot(p, act[...], ((1,), (1,)))
    across = (((1,), (1,)), ((), ()))
    err = lax.dot_general(
        p, feed[...], across, precision=high, preferred_element_type=jnp.float32
    )
    square = jnp.concatenate([p, jnp.zeros((128 - rank, p.shape[1]), p.dtype)], 0)
    gram = lax.dot_general(
        p, square, across, precision=high, preferred_element_type=jnp.float32
    )
    for i in range(out.shape[0]):
        out[i, :, :toks] = u
        out[i, :, toks : toks + rows] = err
        out[i, :, toks + rows :] = gram


def hidden_kernel(got, hid, out, gram):
    toks, rows = hid.shape[1], out.shape[1] // 2
    u = total(got, slice(0, toks))
    err = total(got, slice(toks, toks + rows))
    gram[...] = total(got, slice(toks + rows, None))
    y = exact_dot(u, hid[...], ((1,), (1,)))
    shard = lax.axis_index("x") * lax.axis_size("y") + lax.axis_index("y")
    mine = jnp.where(shard == lax.axis_index("z"), 1.0, 0.0)
    upper = jnp.where(lax.axis_index("c") == 0, mine, 0.0)
    lower = mine - upper
    out[:, :rows] = y[:, :rows] + err * upper
    out[:, rows:] = y[:, rows:] + err * lower


def block_kernel(got, inverse, out):
    rows = total(got, slice(None))
    block = jnp.dot(
        inverse[...], rows, precision=high, preferred_element_type=jnp.float32
    )
    block = block * (1.0 / out.shape[0])
    for i in range(out.shape[0]):
        out[i] = block


def last_kernel(
    blocks, ortho, base, momentum, feed_out, mom_out, q_out, feed_new, mom_new, sems
):
    count, _, rows = blocks.shape
    sends = []
    for i in range(count):
        there = q_out.at[:, pl.ds(i * rows, rows)]
        sends.append(pltpu.make_async_copy(blocks.at[i], there, sems.at[i]))
    for send in sends:
        send.start()
    replica = lax.axis_index("z") * lax.axis_size("c") + lax.axis_index("c")
    mine = blocks[replica]
    part = feed_new.shape[0] // 3
    for i in range(3):
        piece = slice(i * part, (i + 1) * part)
        approx = lax.dot_general(
            mine[:, piece],
            ortho[...],
            (((0,), (0,)), ((), ())),
            precision=high,
            preferred_element_type=jnp.float32,
        )
        feed_new[piece] = base[piece] - approx
        mom_new[piece] = decay_rate * momentum[piece] + approx
        for j, (here, there) in enumerate(((feed_new, feed_out), (mom_new, mom_out))):
            span = pl.ds(i * part, part)
            send = pltpu.make_async_copy(
                here.at[span], there.at[span], sems.at[count + 2 * i + j]
            )
            send.start()
            sends.append(send)
    for send in sends:
        send.wait()


def tie(x, after):
    return lax.optimization_barrier((x, after))[0]


def tree_rounds(nz, nc, nx, ny):
    def device(z, c, x, y):
        return ((z * nc + c) * nx + x) * ny + y

    rounds = []
    known = {c: [(0, 0)] for c in range(nc)}
    steps = ((nx // 2, 0), (0, ny // 2), (nx // 4, 0), (0, ny // 4))
    for step in steps:
        pairs = []
        for c in range(nc):
            dx, dy = step if c == 0 else (step[1], step[0])
            fresh = [((a + dx) % nx, (b + dy) % ny) for a, b in known[c]]
            for z in range(nz):
                ox, oy = z // ny, z % ny
                for (a, b), (e, f) in zip(known[c], fresh):
                    source = device(z, c, (ox + a) % nx, (oy + b) % ny)
                    target = device(z, c, (ox + e) % nx, (oy + f) % ny)
                    pairs.append((source, target))
            known[c] = known[c] + fresh
        rounds.append(pairs)
    return rounds


def per_device(activations, hidden, feedback, momentum, q_start):
    nz, nc, nx, ny = (lax.axis_size(a) for a in ("z", "c", "x", "y"))
    plane = ("x", "y")
    n_dp, n_mp = nz * nc, nx * ny
    z, core = lax.axis_index("z"), lax.axis_index("c")
    replica = z * nc + core
    shard = lax.axis_index("x") * ny + lax.axis_index("y")
    rank = q_start.shape[1]
    cols_mp, toks = hidden.shape
    cols_dp = feedback.shape[0]
    width = activations.shape[1]
    own_start = replica * cols_dp
    root_dev = own_start // cols_mp
    rounds = tree_rounds(nz, nc, nx, ny)
    off_x = (lax.axis_index("x") - z // ny) % nx
    off_y = (lax.axis_index("y") - z % ny) % ny
    first = jnp.where(core == 0, off_x, off_y)
    second = jnp.where(core == 0, off_y, off_x)
    turn = jnp.where(first >= 2, 0, -1)
    turn = jnp.where(second >= 2, 1, turn)
    turn = jnp.where(first % 2 == 1, 2, turn)
    turn = jnp.where(second % 2 == 1, 3, turn)

    def send(held, k):
        return lax.ppermute(held, ("z", "c", "x", "y"), rounds[k])

    def take(held, got, k):
        return jnp.where(turn == k, got, held)

    q_rows = q_start.T
    f32 = jnp.float32
    whole = pl.BlockSpec(memory_space=pltpu.VMEM)
    far = pl.BlockSpec(memory_space=pltpu.HBM)
    token_part, q_owned, held = pl.pallas_call(
        start_kernel,
        out_shape=[
            pltpu.HBM((n_mp, rank, toks), f32),
            pltpu.VMEM((rank, cols_dp), f32),
            pltpu.VMEM((cols_dp, toks), hidden.dtype),
        ],
        in_specs=[far] * 2,
        out_specs=[far, whole, whole],
        scratch_shapes=[
            pltpu.VMEM((rank, cols_mp), f32),
            pltpu.VMEM(hidden.shape, hidden.dtype),
            pltpu.VMEM((rank, toks), f32),
            pltpu.SemaphoreType.DMA((8,)),
            pltpu.SemaphoreType.DMA((n_mp,)),
        ],
        compiler_params=pltpu.CompilerParams(vmem_limit_bytes=4 * 2**20),
        cost_estimate=pl.CostEstimate(
            flops=2 * 10**9, bytes_accessed=3 * 10**6, transcendentals=0
        ),
    )(
        pltpu.with_memory_space_constraint(q_rows, pltpu.HBM),
        pltpu.with_memory_space_constraint(hidden, pltpu.HBM),
    )
    feed_near = near(feedback)
    act_near = activations
    (p_err,) = local(
        early_kernel,
        [pltpu.VMEM((rank, width), f32)],
        1.5,
        near(q_owned),
        feed_near,
    )
    held = tie(held, p_err)
    got = send(held, 0)
    tokens = near(lax.all_to_all(token_part, plane, 0, 0))
    (p_part,) = local(
        left_kernel,
        [pltpu.VMEM((rank, width), f32)],
        1,
        tokens,
        near(act_near),
        near(p_err),
    )
    p_pair = lax.all_gather(p_part, "c").sum(0)
    held = take(held, tie(got, p_pair), 0)
    got = send(held, 1)
    part = rank // nc
    p_pair = lax.dynamic_slice_in_dim(p_pair, core * part, part, 0)
    p_half = copies(p_pair, "z", nz).sum(0)
    held = take(held, got, 1)
    got = send(held, 2)
    p_sum = lax.all_gather(p_half, "c", tiled=True)

    (packed,) = local(
        right_kernel,
        [pltpu.VMEM((n_mp, rank, toks + cols_dp + 128), f32)],
        2,
        near(p_sum),
        near(act_near),
        feed_near,
    )
    packed = near(lax.all_to_all(packed, plane, 0, 0))
    hid, gram_mat = local(
        hidden_kernel,
        [pltpu.VMEM((rank, cols_mp), f32), pltpu.VMEM((rank, 128), f32)],
        1,
        packed,
        near(hidden),
    )
    gram_mat = gram_mat[:, :rank]
    half = lax.all_gather(hid, "c").sum(0)
    half = lax.dynamic_slice_in_dim(half, core * cols_dp, cols_dp, 1)
    held = take(held, tie(got, half), 2)
    got = send(held, 3)
    gram_mat = tie(gram_mat, held)
    factor = jnp.linalg.cholesky(gram_mat)
    inverse = lax.linalg.triangular_solve(
        factor, jnp.eye(rank, dtype=jnp.float32), left_side=True, lower=True
    )
    half = near(copies(half, "z", nz))
    (block,) = local(
        block_kernel,
        [pltpu.VMEM((n_dp, rank, cols_dp), f32)],
        1,
        half,
        near(inverse),
    )
    held = take(held, tie(got, block), 3)
    own_grad = jnp.dot(held, act_near, preferred_element_type=jnp.float32)
    base = lax.optimization_barrier(own_grad + feedback)
    blocks = near(lax.all_to_all(block, ("x", "y", "c"), 0, 0))
    ortho = jnp.dot(inverse, p_sum, precision=high)
    new_feedback, new_momentum, q_next = pl.pallas_call(
        last_kernel,
        out_shape=[
            pltpu.HBM(feedback.shape, f32),
            pltpu.HBM(momentum.shape, f32),
            pltpu.HBM(q_rows.shape, f32),
        ],
        in_specs=[whole] * 4,
        out_specs=[far] * 3,
        scratch_shapes=[
            pltpu.VMEM(feedback.shape, f32),
            pltpu.VMEM(momentum.shape, f32),
            pltpu.SemaphoreType.DMA((n_dp + 6,)),
        ],
        compiler_params=pltpu.CompilerParams(vmem_limit_bytes=4 * 2**20),
        cost_estimate=pl.CostEstimate(
            flops=2 * 10**9, bytes_accessed=3 * 10**6, transcendentals=0
        ),
    )(blocks, near(ortho), near(base), near(momentum))
    return (new_feedback, new_momentum, q_next.T)


def solution(mesh):
    grid = Mesh(mesh.devices.reshape(16, 2, 4, 4), ("z", "c", "x", "y"))
    dp, mp = ("z", "c"), ("x", "y")
    placed = (P(dp, mp), P(mp, dp), P(dp, mp), P(dp, mp), P())
    return jax.shard_map(
        per_device,
        mesh=grid,
        in_specs=placed,
        out_specs=(P(dp, mp), P(dp, mp), P()),
        check_vma=False,
    )
```

```python
import jax
import jax.numpy as jnp
from jax import lax
from jax.experimental import pallas as pl
from jax.experimental.pallas import tpu as pltpu
from jax.sharding import Mesh, PartitionSpec as P

decay_rate = 0.9
high = lax.Precision.HIGHEST


def copies(x, axes, count):
    return lax.all_to_all(jnp.broadcast_to(x[None], (count,) + x.shape), axes, 0, 0)


def near(x):
    return pltpu.with_memory_space_constraint(x, pltpu.VMEM)


def local(kernel, outs, micros, *args):
    whole = pl.BlockSpec(memory_space=pltpu.VMEM)
    size = sum(a.size * a.dtype.itemsize for a in args)
    return pl.pallas_call(
        kernel,
        out_shape=outs,
        in_specs=[whole] * len(args),
        out_specs=[whole] * len(outs),
        compiler_params=pltpu.CompilerParams(vmem_limit_bytes=4 * 2**20),
        cost_estimate=pl.CostEstimate(
            flops=int(micros * 4e9), bytes_accessed=size, transcendentals=0
        ),
    )(*args)


def exact_dot(x, wide, dims):
    y = lax.dot_general(
        parts_of(x), wide, (dims, ((), ())), preferred_element_type=jnp.float32
    )
    n = x.shape[0]
    return (y[2 * n : 3 * n] + y[n : 2 * n]) + y[:n]


def total(ref, lanes):
    y = ref[0, :, lanes]
    for i in range(1, ref.shape[0]):
        y = y + ref[i, :, lanes]
    return y


def three(x):
    a = x.astype(jnp.bfloat16).astype(jnp.float32)
    r = x - a
    b = r.astype(jnp.bfloat16).astype(jnp.float32)
    return a, b, r - b


def parts_of(x):
    return jnp.concatenate([*three(x), jnp.zeros_like(x)], 0).astype(jnp.bfloat16)


def start_kernel(q, hid, out, q_own, piece_out, q_near, held, row, sems, done):
    rows, own_rows = hid.shape[0], q_own.shape[1]
    count = sems.shape[0] - 2
    step = rows // count
    shard = lax.axis_index("x") * lax.axis_size("y") + lax.axis_index("y")
    replica = lax.axis_index("z") * lax.axis_size("c") + lax.axis_index("c")
    mine = q.at[:, pl.ds(pl.multiple_of(shard * rows, rows), rows)]
    own = q.at[:, pl.ds(pl.multiple_of(replica * own_rows, own_rows), own_rows)]
    first = pltpu.make_async_copy(mine, q_near, sems.at[count])
    last = pltpu.make_async_copy(own, q_own, sems.at[count + 1])
    loads = []
    for i in range(count):
        piece = pl.ds(i * step, step)
        loads.append(pltpu.make_async_copy(hid.at[piece], held.at[piece], sems.at[i]))
    for load in [first] + loads + [last]:
        load.start()
    first.wait()
    parts = parts_of(q_near[...])
    y = jnp.zeros((parts.shape[0], hid.shape[1]), jnp.float32)
    for i in range(count):
        loads[i].wait()
        y = y + jnp.dot(
            parts[:, i * step : (i + 1) * step],
            held[i * step : (i + 1) * step, :],
            preferred_element_type=jnp.float32,
        )
    n = row.shape[0]
    row[...] = (y[2 * n : 3 * n] + y[n : 2 * n]) + y[:n]
    sends = [
        pltpu.make_async_copy(row, out.at[i], done.at[i]) for i in range(out.shape[0])
    ]
    for send in sends:
        send.start()
    core = lax.axis_index("c")
    piece_out[...] = held[pl.ds(pl.multiple_of(core * own_rows, own_rows), own_rows), :]
    last.wait()
    for send in sends:
        send.wait()


def early_kernel(q, feed, err):
    err[...] = jnp.dot(
        q[...], feed[...], precision=high, preferred_element_type=jnp.float32
    )


def left_kernel(got, act, err, out):
    tokens = total(got, slice(None))
    out[...] = exact_dot(tokens, act[...], ((1,), (0,))) + err[...]


def right_kernel(p_ref, act, feed, out):
    p = p_ref[...]
    rank, toks = p.shape[0], act.shape[0]
    rows = feed.shape[0]
    across = (((1,), (1,)), ((), ()))
    parts = parts_of(p)
    y = lax.dot_general(
        parts, act[...], across, preferred_element_type=jnp.float32
    )
    n = rank
    u = (y[2 * n : 3 * n] + y[n : 2 * n]) + y[:n]
    e, f, g = (
        lax.dot_general(
            parts, v.astype(jnp.bfloat16), across, preferred_element_type=jnp.float32
        )
        for v in three(feed[...])
    )
    small = (g[:n] + f[n : 2 * n]) + e[2 * n : 3 * n]
    err = (small + (f[:n] + e[n : 2 * n])) + e[:n]
    lane = lax.broadcasted_iota(jnp.int32, (rank, 128), 1)
    gram = jnp.zeros((rank, 128), jnp.float32)
    for i in range(rank):
        column = jnp.sum(p * p[i : i + 1], axis=1, keepdims=True)
        gram = jnp.where(lane == i, column, gram)
    for i in range(out.shape[0]):
        out[i, :, :toks] = u
        out[i, :, toks : toks + rows] = err
        out[i, :, toks + rows :] = gram


def hidden_kernel(got, hid, out, gram):
    toks, rows = hid.shape[1], out.shape[1] // 2
    u = total(got, slice(0, toks))
    err = total(got, slice(toks, toks + rows))
    gram[...] = total(got, slice(toks + rows, None))
    y = exact_dot(u, hid[...], ((1,), (1,)))
    shard = lax.axis_index("x") * lax.axis_size("y") + lax.axis_index("y")
    mine = jnp.where(shard == lax.axis_index("z"), 1.0, 0.0)
    upper = jnp.where(lax.axis_index("c") == 0, mine, 0.0)
    lower = mine - upper
    out[:, :rows] = y[:, :rows] + err * upper
    out[:, rows:] = y[:, rows:] + err * lower


def block_kernel(got, inverse, out):
    rows = total(got, slice(None))
    inv = inverse[...]
    block = inv[:, 0:1] * rows[0:1]
    for i in range(1, rows.shape[0]):
        block = block + inv[:, i : i + 1] * rows[i : i + 1]
    block = block * (1.0 / out.shape[0])
    for i in range(out.shape[0]):
        out[i] = block


def last_kernel(
    blocks, ortho, base, momentum, feed_out, mom_out, q_out, feed_new, mom_new, sems
):
    count, _, rows = blocks.shape
    sends = []
    for i in range(count):
        there = q_out.at[:, pl.ds(i * rows, rows)]
        sends.append(pltpu.make_async_copy(blocks.at[i], there, sems.at[i]))
    for send in sends:
        send.start()
    replica = lax.axis_index("z") * lax.axis_size("c") + lax.axis_index("c")
    a, b, c = three(blocks[replica])
    left = jnp.concatenate([c, b, a, b, a, a], 0).astype(jnp.bfloat16)
    a, b, c = three(ortho[...])
    right = jnp.concatenate([a, b, c, a, b, a], 0).astype(jnp.bfloat16)
    part = feed_new.shape[0] // 3
    for i in range(3):
        piece = slice(i * part, (i + 1) * part)
        approx = lax.dot_general(
            left[:, piece],
            right,
            (((0,), (0,)), ((), ())),
            preferred_element_type=jnp.float32,
        )
        feed_new[piece] = base[piece] - approx
        mom_new[piece] = decay_rate * momentum[piece] + approx
        for j, (here, there) in enumerate(((feed_new, feed_out), (mom_new, mom_out))):
            span = pl.ds(i * part, part)
            send = pltpu.make_async_copy(
                here.at[span], there.at[span], sems.at[count + 2 * i + j]
            )
            send.start()
            sends.append(send)
    for send in sends:
        send.wait()


def tie(x, after):
    return lax.optimization_barrier((x, after))[0]


def tree_rounds(nz, nc, nx, ny):
    def device(z, c, x, y):
        return ((z * nc + c) * nx + x) * ny + y

    rounds = []
    known = {c: [(0, 0)] for c in range(nc)}
    steps = ((nx // 2, 0), (0, ny // 2), (nx // 4, 0), (0, ny // 4))
    for step in steps:
        pairs = []
        for c in range(nc):
            dx, dy = step if c == 0 else (step[1], step[0])
            fresh = [((a + dx) % nx, (b + dy) % ny) for a, b in known[c]]
            for z in range(nz):
                ox, oy = z // ny, z % ny
                for (a, b), (e, f) in zip(known[c], fresh):
                    source = device(z, c, (ox + a) % nx, (oy + b) % ny)
                    target = device(z, c, (ox + e) % nx, (oy + f) % ny)
                    pairs.append((source, target))
            known[c] = known[c] + fresh
        rounds.append(pairs)
    return rounds


def per_device(activations, hidden, feedback, momentum, q_start):
    nz, nc, nx, ny = (lax.axis_size(a) for a in ("z", "c", "x", "y"))
    plane = ("x", "y")
    n_dp, n_mp = nz * nc, nx * ny
    z, core = lax.axis_index("z"), lax.axis_index("c")
    replica = z * nc + core
    shard = lax.axis_index("x") * ny + lax.axis_index("y")
    rank = q_start.shape[1]
    cols_mp, toks = hidden.shape
    cols_dp = feedback.shape[0]
    width = activations.shape[1]
    own_start = replica * cols_dp
    root_dev = own_start // cols_mp
    rounds = tree_rounds(nz, nc, nx, ny)
    off_x = (lax.axis_index("x") - z // ny) % nx
    off_y = (lax.axis_index("y") - z % ny) % ny
    first = jnp.where(core == 0, off_x, off_y)
    second = jnp.where(core == 0, off_y, off_x)
    turn = jnp.where(first >= 2, 0, -1)
    turn = jnp.where(second >= 2, 1, turn)
    turn = jnp.where(first % 2 == 1, 2, turn)
    turn = jnp.where(second % 2 == 1, 3, turn)

    def send(held, k):
        return lax.ppermute(held, ("z", "c", "x", "y"), rounds[k])

    def take(held, got, k):
        return jnp.where(turn == k, got, held)

    q_rows = q_start.T
    f32 = jnp.float32
    whole = pl.BlockSpec(memory_space=pltpu.VMEM)
    far = pl.BlockSpec(memory_space=pltpu.HBM)
    token_part, q_owned, held = pl.pallas_call(
        start_kernel,
        out_shape=[
            pltpu.HBM((n_mp, rank, toks), f32),
            pltpu.VMEM((rank, cols_dp), f32),
            pltpu.VMEM((cols_dp, toks), hidden.dtype),
        ],
        in_specs=[far] * 2,
        out_specs=[far, whole, whole],
        scratch_shapes=[
            pltpu.VMEM((rank, cols_mp), f32),
            pltpu.VMEM(hidden.shape, hidden.dtype),
            pltpu.VMEM((rank, toks), f32),
            pltpu.SemaphoreType.DMA((8,)),
            pltpu.SemaphoreType.DMA((n_mp,)),
        ],
        compiler_params=pltpu.CompilerParams(vmem_limit_bytes=4 * 2**20),
        cost_estimate=pl.CostEstimate(
            flops=2 * 10**9, bytes_accessed=3 * 10**6, transcendentals=0
        ),
    )(
        pltpu.with_memory_space_constraint(q_rows, pltpu.HBM),
        pltpu.with_memory_space_constraint(hidden, pltpu.HBM),
    )
    feed_near = near(feedback)
    act_near = activations
    (p_err,) = local(
        early_kernel,
        [pltpu.VMEM((rank, width), f32)],
        1.5,
        near(q_owned),
        feed_near,
    )
    held = tie(held, p_err)
    got = send(held, 0)
    tokens = near(lax.all_to_all(token_part, plane, 0, 0))
    (p_part,) = local(
        left_kernel,
        [pltpu.VMEM((rank, width), f32)],
        1,
        tokens,
        near(act_near),
        near(p_err),
    )
    p_pair = lax.all_gather(p_part, "c").sum(0)
    held = take(held, tie(got, p_pair), 0)
    got = send(held, 1)
    part = rank // nc
    p_pair = lax.dynamic_slice_in_dim(p_pair, core * part, part, 0)
    p_half = copies(p_pair, "z", nz).sum(0)
    held = take(held, got, 1)
    got = send(held, 2)
    p_sum = lax.all_gather(p_half, "c", tiled=True)

    (packed,) = local(
        right_kernel,
        [pltpu.VMEM((n_mp, rank, toks + cols_dp + 128), f32)],
        2,
        near(p_sum),
        near(act_near),
        feed_near,
    )
    packed = near(lax.all_to_all(packed, plane, 0, 0))
    hid, gram_mat = local(
        hidden_kernel,
        [pltpu.VMEM((rank, cols_mp), f32), pltpu.VMEM((rank, 128), f32)],
        1,
        packed,
        near(hidden),
    )
    gram_mat = gram_mat[:, :rank]
    half = lax.all_gather(hid, "c").sum(0)
    half = lax.dynamic_slice_in_dim(half, core * cols_dp, cols_dp, 1)
    held = take(held, tie(got, half), 2)
    got = send(held, 3)
    gram_mat = tie(gram_mat, held)
    factor = jnp.linalg.cholesky(gram_mat)
    inverse = lax.linalg.triangular_solve(
        factor, jnp.eye(rank, dtype=jnp.float32), left_side=True, lower=True
    )
    half = near(copies(half, "z", nz))
    (block,) = local(
        block_kernel,
        [pltpu.VMEM((n_dp, rank, cols_dp), f32)],
        1,
        half,
        near(inverse),
    )
    held = take(held, tie(got, block), 3)
    own_grad = jnp.dot(held, act_near, preferred_element_type=jnp.float32)
    base = lax.optimization_barrier(own_grad + feedback)
    blocks = near(lax.all_to_all(block, ("x", "y", "c"), 0, 0))
    ortho = jnp.dot(inverse, p_sum, precision=high)
    new_feedback, new_momentum, q_next = pl.pallas_call(
        last_kernel,
        out_shape=[
            pltpu.HBM(feedback.shape, f32),
            pltpu.HBM(momentum.shape, f32),
            pltpu.HBM(q_rows.shape, f32),
        ],
        in_specs=[whole] * 4,
        out_specs=[far] * 3,
        scratch_shapes=[
            pltpu.VMEM(feedback.shape, f32),
            pltpu.VMEM(momentum.shape, f32),
            pltpu.SemaphoreType.DMA((n_dp + 6,)),
        ],
        compiler_params=pltpu.CompilerParams(vmem_limit_bytes=4 * 2**20),
        cost_estimate=pl.CostEstimate(
            flops=2 * 10**9, bytes_accessed=3 * 10**6, transcendentals=0
        ),
    )(blocks, near(ortho), near(base), near(momentum))
    return (new_feedback, new_momentum, q_next.T)


def solution(mesh):
    grid = Mesh(mesh.devices.reshape(16, 2, 4, 4), ("z", "c", "x", "y"))
    dp, mp = ("z", "c"), ("x", "y")
    placed = (P(dp, mp), P(mp, dp), P(dp, mp), P(dp, mp), P())
    return jax.shard_map(
        per_device,
        mesh=grid,
        in_specs=placed,
        out_specs=(P(dp, mp), P(dp, mp), P()),
        check_vma=False,
    )
```

```python
import jax
import jax.numpy as jnp
from jax import lax
from jax.experimental import pallas as pl
from jax.experimental.pallas import tpu as pltpu
from jax.sharding import Mesh, PartitionSpec as P

decay_rate = 0.9
high = lax.Precision.HIGHEST


def copies(x, axes, count):
    return lax.all_to_all(jnp.broadcast_to(x[None], (count,) + x.shape), axes, 0, 0)


def near(x):
    return pltpu.with_memory_space_constraint(x, pltpu.VMEM)


def local(kernel, outs, micros, *args):
    whole = pl.BlockSpec(memory_space=pltpu.VMEM)
    size = sum(a.size * a.dtype.itemsize for a in args)
    return pl.pallas_call(
        kernel,
        out_shape=outs,
        in_specs=[whole] * len(args),
        out_specs=[whole] * len(outs),
        compiler_params=pltpu.CompilerParams(vmem_limit_bytes=4 * 2**20),
        cost_estimate=pl.CostEstimate(
            flops=int(micros * 4e9), bytes_accessed=size, transcendentals=0
        ),
    )(*args)


def exact_dot(x, wide, dims):
    y = lax.dot_general(
        parts_of(x), wide, (dims, ((), ())), preferred_element_type=jnp.float32
    )
    n = x.shape[0]
    return (y[2 * n : 3 * n] + y[n : 2 * n]) + y[:n]


def total(ref, lanes):
    y = ref[0, :, lanes]
    for i in range(1, ref.shape[0]):
        y = y + ref[i, :, lanes]
    return y


def three(x):
    a = x.astype(jnp.bfloat16).astype(jnp.float32)
    r = x - a
    b = r.astype(jnp.bfloat16).astype(jnp.float32)
    return a, b, r - b


def parts_of(x):
    return jnp.concatenate([*three(x), jnp.zeros_like(x)], 0).astype(jnp.bfloat16)


def start_kernel(q, hid, out, q_own, piece_out, q_near, held, row, sems, done):
    rows, own_rows = hid.shape[0], q_own.shape[1]
    count = sems.shape[0] - 2
    step = rows // count
    shard = lax.axis_index("x") * lax.axis_size("y") + lax.axis_index("y")
    replica = lax.axis_index("z") * lax.axis_size("c") + lax.axis_index("c")
    mine = q.at[:, pl.ds(pl.multiple_of(shard * rows, rows), rows)]
    own = q.at[:, pl.ds(pl.multiple_of(replica * own_rows, own_rows), own_rows)]
    first = pltpu.make_async_copy(mine, q_near, sems.at[count])
    last = pltpu.make_async_copy(own, q_own, sems.at[count + 1])
    loads = []
    for i in range(count):
        piece = pl.ds(i * step, step)
        loads.append(pltpu.make_async_copy(hid.at[piece], held.at[piece], sems.at[i]))
    for load in [first] + loads + [last]:
        load.start()
    first.wait()
    parts = parts_of(q_near[...])
    y = jnp.zeros((parts.shape[0], hid.shape[1]), jnp.float32)
    for i in range(count):
        loads[i].wait()
        y = y + jnp.dot(
            parts[:, i * step : (i + 1) * step],
            held[i * step : (i + 1) * step, :],
            preferred_element_type=jnp.float32,
        )
    n = row.shape[0]
    row[...] = (y[2 * n : 3 * n] + y[n : 2 * n]) + y[:n]
    sends = [
        pltpu.make_async_copy(row, out.at[i], done.at[i]) for i in range(out.shape[0])
    ]
    for send in sends:
        send.start()
    core = lax.axis_index("c")
    piece_out[...] = held[pl.ds(pl.multiple_of(core * own_rows, own_rows), own_rows), :]
    last.wait()
    for send in sends:
        send.wait()


def early_kernel(q, feed, err):
    err[...] = jnp.dot(
        q[...], feed[...], precision=high, preferred_element_type=jnp.float32
    )


def left_kernel(got, act, err, out):
    tokens = total(got, slice(None))
    out[...] = exact_dot(tokens, act[...], ((1,), (0,))) + err[...]


def right_kernel(p_ref, act, feed, out):
    p = p_ref[...]
    rank, toks = p.shape[0], act.shape[0]
    rows = feed.shape[0]
    across = (((1,), (1,)), ((), ()))
    parts = parts_of(p)
    y = lax.dot_general(
        parts, act[...], across, preferred_element_type=jnp.float32
    )
    n = rank
    u = (y[2 * n : 3 * n] + y[n : 2 * n]) + y[:n]
    e, f, g = (
        lax.dot_general(
            parts, v.astype(jnp.bfloat16), across, preferred_element_type=jnp.float32
        )
        for v in three(feed[...])
    )
    small = (g[:n] + f[n : 2 * n]) + e[2 * n : 3 * n]
    err = (small + (f[:n] + e[n : 2 * n])) + e[:n]
    lane = lax.broadcasted_iota(jnp.int32, (rank, 128), 1)
    gram = jnp.zeros((rank, 128), jnp.float32)
    for i in range(rank):
        column = jnp.sum(p * p[i : i + 1], axis=1, keepdims=True)
        gram = jnp.where(lane == i, column, gram)
    for i in range(out.shape[0]):
        out[i, :, :toks] = u
        out[i, :, toks : toks + rows] = err
        out[i, :, toks + rows :] = gram


def hidden_kernel(got, hid, low, out, gram):
    toks, rows = hid.shape[1], out.shape[1] // 2
    u = total(got, slice(0, toks))
    err = total(got, slice(toks, toks + rows))
    gram[...] = total(got, slice(toks + rows, None))
    parts = parts_of(u)
    shard = lax.axis_index("x") * lax.axis_size("y") + lax.axis_index("y")
    mine = jnp.where(shard == lax.axis_index("z"), 1.0, 0.0)
    upper = jnp.where(lax.axis_index("c") == 0, mine, 0.0)
    lower = mine - upper
    n = out.shape[0]
    for i, (half, weight) in enumerate(((hid, upper), (low, lower))):
        y = lax.dot_general(
            parts,
            half[...],
            (((1,), (1,)), ((), ())),
            preferred_element_type=jnp.float32,
        )
        y = (y[2 * n : 3 * n] + y[n : 2 * n]) + y[:n]
        out[:, i * rows : (i + 1) * rows] = y + err * weight


def block_kernel(got, inverse, out):
    rows = total(got, slice(None))
    inv = inverse[...]
    block = inv[:, 0:1] * rows[0:1]
    for i in range(1, rows.shape[0]):
        block = block + inv[:, i : i + 1] * rows[i : i + 1]
    block = block * (1.0 / out.shape[0])
    for i in range(out.shape[0]):
        out[i] = block


def last_kernel(
    blocks, ortho, base, momentum, feed_out, mom_out, q_out, feed_new, mom_new, sems
):
    count, _, rows = blocks.shape
    sends = []
    for i in range(count):
        there = q_out.at[:, pl.ds(i * rows, rows)]
        sends.append(pltpu.make_async_copy(blocks.at[i], there, sems.at[i]))
    for send in sends:
        send.start()
    replica = lax.axis_index("z") * lax.axis_size("c") + lax.axis_index("c")
    a, b, c = three(blocks[replica])
    left = jnp.concatenate([c, b, a, b, a, a], 0).astype(jnp.bfloat16)
    a, b, c = three(ortho[...])
    right = jnp.concatenate([a, b, c, a, b, a], 0).astype(jnp.bfloat16)
    part = feed_new.shape[0] // 3
    for i in range(3):
        piece = slice(i * part, (i + 1) * part)
        approx = lax.dot_general(
            left[:, piece],
            right,
            (((0,), (0,)), ((), ())),
            preferred_element_type=jnp.float32,
        )
        feed_new[piece] = base[piece] - approx
        mom_new[piece] = decay_rate * momentum[piece] + approx
        for j, (here, there) in enumerate(((feed_new, feed_out), (mom_new, mom_out))):
            span = pl.ds(i * part, part)
            send = pltpu.make_async_copy(
                here.at[span], there.at[span], sems.at[count + 2 * i + j]
            )
            send.start()
            sends.append(send)
    for send in sends:
        send.wait()


def tie(x, after):
    return lax.optimization_barrier((x, after))[0]


def tree_rounds(nz, nc, nx, ny):
    def device(z, c, x, y):
        return ((z * nc + c) * nx + x) * ny + y

    rounds = []
    known = {c: [(0, 0)] for c in range(nc)}
    steps = ((nx // 2, 0), (0, ny // 2), (nx // 4, 0), (0, ny // 4))
    for step in steps:
        pairs = []
        for c in range(nc):
            dx, dy = step if c == 0 else (step[1], step[0])
            fresh = [((a + dx) % nx, (b + dy) % ny) for a, b in known[c]]
            for z in range(nz):
                ox, oy = z // ny, z % ny
                for (a, b), (e, f) in zip(known[c], fresh):
                    source = device(z, c, (ox + a) % nx, (oy + b) % ny)
                    target = device(z, c, (ox + e) % nx, (oy + f) % ny)
                    pairs.append((source, target))
            known[c] = known[c] + fresh
        rounds.append(pairs)
    return rounds


def per_device(activations, hidden, feedback, momentum, q_start):
    nz, nc, nx, ny = (lax.axis_size(a) for a in ("z", "c", "x", "y"))
    plane = ("x", "y")
    n_dp, n_mp = nz * nc, nx * ny
    z, core = lax.axis_index("z"), lax.axis_index("c")
    replica = z * nc + core
    shard = lax.axis_index("x") * ny + lax.axis_index("y")
    rank = q_start.shape[1]
    cols_mp, toks = hidden.shape
    cols_dp = feedback.shape[0]
    width = activations.shape[1]
    own_start = replica * cols_dp
    root_dev = own_start // cols_mp
    rounds = tree_rounds(nz, nc, nx, ny)
    off_x = (lax.axis_index("x") - z // ny) % nx
    off_y = (lax.axis_index("y") - z % ny) % ny
    first = jnp.where(core == 0, off_x, off_y)
    second = jnp.where(core == 0, off_y, off_x)
    turn = jnp.where(first >= 2, 0, -1)
    turn = jnp.where(second >= 2, 1, turn)
    turn = jnp.where(first % 2 == 1, 2, turn)
    turn = jnp.where(second % 2 == 1, 3, turn)

    def send(held, k):
        return lax.ppermute(held, ("z", "c", "x", "y"), rounds[k])

    def take(held, got, k):
        return jnp.where(turn == k, got, held)

    q_rows = q_start.T
    f32 = jnp.float32
    whole = pl.BlockSpec(memory_space=pltpu.VMEM)
    far = pl.BlockSpec(memory_space=pltpu.HBM)
    token_part, q_owned, held = pl.pallas_call(
        start_kernel,
        out_shape=[
            pltpu.HBM((n_mp, rank, toks), f32),
            pltpu.VMEM((rank, cols_dp), f32),
            pltpu.VMEM((cols_dp, toks), hidden.dtype),
        ],
        in_specs=[far] * 2,
        out_specs=[far, whole, whole],
        scratch_shapes=[
            pltpu.VMEM((rank, cols_mp), f32),
            pltpu.VMEM(hidden.shape, hidden.dtype),
            pltpu.VMEM((rank, toks), f32),
            pltpu.SemaphoreType.DMA((8,)),
            pltpu.SemaphoreType.DMA((n_mp,)),
        ],
        compiler_params=pltpu.CompilerParams(vmem_limit_bytes=4 * 2**20),
        cost_estimate=pl.CostEstimate(
            flops=2 * 10**9, bytes_accessed=3 * 10**6, transcendentals=0
        ),
    )(
        pltpu.with_memory_space_constraint(q_rows, pltpu.HBM),
        pltpu.with_memory_space_constraint(hidden, pltpu.HBM),
    )
    feed_near = near(feedback)
    act_near = activations
    (p_err,) = local(
        early_kernel,
        [pltpu.VMEM((rank, width), f32)],
        1.5,
        near(q_owned),
        feed_near,
    )
    held = tie(held, p_err)
    got = send(held, 0)
    tokens = near(lax.all_to_all(token_part, plane, 0, 0))
    (p_part,) = local(
        left_kernel,
        [pltpu.VMEM((rank, width), f32)],
        1,
        tokens,
        near(act_near),
        near(p_err),
    )
    p_pair = lax.all_gather(p_part, "c").sum(0)
    held = take(held, tie(got, p_pair), 0)
    got = send(held, 1)
    part = rank // nc
    p_pair = lax.dynamic_slice_in_dim(p_pair, core * part, part, 0)
    p_half = copies(p_pair, "z", nz).sum(0)
    held = take(held, got, 1)
    got = send(held, 2)
    p_sum = lax.all_gather(p_half, "c", tiled=True)

    (packed,) = local(
        right_kernel,
        [pltpu.VMEM((n_mp, rank, toks + cols_dp + 128), f32)],
        2,
        near(p_sum),
        near(act_near),
        feed_near,
    )
    hid_late = tie(hidden, packed)
    hid_top, hid_low = hid_late[:cols_dp], hid_late[cols_dp:]
    packed = near(lax.all_to_all(packed, plane, 0, 0))
    hid, gram_mat = local(
        hidden_kernel,
        [pltpu.VMEM((rank, cols_mp), f32), pltpu.VMEM((rank, 128), f32)],
        1,
        packed,
        near(hid_top),
        near(hid_low),
    )
    gram_mat = gram_mat[:, :rank]
    half = lax.all_gather(hid, "c").sum(0)
    half = lax.dynamic_slice_in_dim(half, core * cols_dp, cols_dp, 1)
    held = take(held, tie(got, half), 2)
    got = send(held, 3)
    gram_mat = tie(gram_mat, held)
    factor = jnp.linalg.cholesky(gram_mat)
    inverse = lax.linalg.triangular_solve(
        factor, jnp.eye(rank, dtype=jnp.float32), left_side=True, lower=True
    )
    half = near(copies(half, "z", nz))
    (block,) = local(
        block_kernel,
        [pltpu.VMEM((n_dp, rank, cols_dp), f32)],
        1,
        half,
        near(inverse),
    )
    held = take(held, tie(got, block), 3)
    own_grad = jnp.dot(held, act_near, preferred_element_type=jnp.float32)
    base = lax.optimization_barrier(own_grad + feedback)
    blocks = near(lax.all_to_all(block, ("x", "y", "c"), 0, 0))
    ortho = jnp.dot(inverse, p_sum, precision=high)
    new_feedback, new_momentum, q_next = pl.pallas_call(
        last_kernel,
        out_shape=[
            pltpu.HBM(feedback.shape, f32),
            pltpu.HBM(momentum.shape, f32),
            pltpu.HBM(q_rows.shape, f32),
        ],
        in_specs=[whole] * 4,
        out_specs=[far] * 3,
        scratch_shapes=[
            pltpu.VMEM(feedback.shape, f32),
            pltpu.VMEM(momentum.shape, f32),
            pltpu.SemaphoreType.DMA((n_dp + 6,)),
        ],
        compiler_params=pltpu.CompilerParams(vmem_limit_bytes=4 * 2**20),
        cost_estimate=pl.CostEstimate(
            flops=2 * 10**9, bytes_accessed=3 * 10**6, transcendentals=0
        ),
    )(blocks, near(ortho), near(base), near(momentum))
    return (new_feedback, new_momentum, q_next.T)


def solution(mesh):
    grid = Mesh(mesh.devices.reshape(16, 2, 4, 4), ("z", "c", "x", "y"))
    dp, mp = ("z", "c"), ("x", "y")
    placed = (P(dp, mp), P(mp, dp), P(dp, mp), P(dp, mp), P())
    return jax.shard_map(
        per_device,
        mesh=grid,
        in_specs=placed,
        out_specs=(P(dp, mp), P(dp, mp), P()),
        check_vma=False,
    )
```

```python
import jax
import jax.numpy as jnp
from jax import lax
from jax.experimental import pallas as pl
from jax.experimental.pallas import tpu as pltpu
from jax.sharding import Mesh, PartitionSpec as P

decay_rate = 0.9
high = lax.Precision.HIGHEST


def copies(x, axes, count):
    return lax.all_to_all(jnp.broadcast_to(x[None], (count,) + x.shape), axes, 0, 0)


def near(x):
    return pltpu.with_memory_space_constraint(x, pltpu.VMEM)


def local(kernel, outs, micros, *args):
    whole = pl.BlockSpec(memory_space=pltpu.VMEM)
    size = sum(a.size * a.dtype.itemsize for a in args)
    return pl.pallas_call(
        kernel,
        out_shape=outs,
        in_specs=[whole] * len(args),
        out_specs=[whole] * len(outs),
        compiler_params=pltpu.CompilerParams(vmem_limit_bytes=4 * 2**20),
        cost_estimate=pl.CostEstimate(
            flops=int(micros * 4e9), bytes_accessed=size, transcendentals=0
        ),
    )(*args)


def exact_dot(x, wide, dims):
    y = lax.dot_general(
        parts_of(x), wide, (dims, ((), ())), preferred_element_type=jnp.float32
    )
    n = x.shape[0]
    return (y[2 * n : 3 * n] + y[n : 2 * n]) + y[:n]


def total(ref, lanes):
    y = ref[0, :, lanes]
    for i in range(1, ref.shape[0]):
        y = y + ref[i, :, lanes]
    return y


def three(x):
    a = x.astype(jnp.bfloat16).astype(jnp.float32)
    r = x - a
    b = r.astype(jnp.bfloat16).astype(jnp.float32)
    return a, b, r - b


def parts_of(x):
    return jnp.concatenate([*three(x), jnp.zeros_like(x)], 0).astype(jnp.bfloat16)


def start_kernel(q, hid, out, q_own, piece_out, q_near, held, row, sems, done):
    rows, own_rows = hid.shape[0], q_own.shape[1]
    count = sems.shape[0] - 2
    step = rows // count
    shard = lax.axis_index("x") * lax.axis_size("y") + lax.axis_index("y")
    replica = lax.axis_index("z") * lax.axis_size("c") + lax.axis_index("c")
    mine = q.at[:, pl.ds(pl.multiple_of(shard * rows, rows), rows)]
    own = q.at[:, pl.ds(pl.multiple_of(replica * own_rows, own_rows), own_rows)]
    first = pltpu.make_async_copy(mine, q_near, sems.at[count])
    last = pltpu.make_async_copy(own, q_own, sems.at[count + 1])
    loads = []
    for i in range(count):
        piece = pl.ds(i * step, step)
        loads.append(pltpu.make_async_copy(hid.at[piece], held.at[piece], sems.at[i]))
    for load in [first] + loads + [last]:
        load.start()
    first.wait()
    parts = parts_of(q_near[...])
    y = jnp.zeros((parts.shape[0], hid.shape[1]), jnp.float32)
    for i in range(count):
        loads[i].wait()
        y = y + jnp.dot(
            parts[:, i * step : (i + 1) * step],
            held[i * step : (i + 1) * step, :],
            preferred_element_type=jnp.float32,
        )
    n = row.shape[0]
    row[...] = (y[2 * n : 3 * n] + y[n : 2 * n]) + y[:n]
    sends = [
        pltpu.make_async_copy(row, out.at[i], done.at[i]) for i in range(out.shape[0])
    ]
    for send in sends:
        send.start()
    core = lax.axis_index("c")
    piece_out[...] = held[pl.ds(pl.multiple_of(core * own_rows, own_rows), own_rows), :]
    last.wait()
    for send in sends:
        send.wait()


def early_kernel(q, feed, err):
    err[...] = jnp.dot(
        q[...], feed[...], precision=high, preferred_element_type=jnp.float32
    )


def left_kernel(got, act, err, out):
    tokens = total(got, slice(None))
    out[...] = exact_dot(tokens, act[...], ((1,), (0,))) + err[...]


def right_kernel(p_ref, act, feed, out):
    p = p_ref[...]
    rank, toks = p.shape[0], act.shape[0]
    rows = feed.shape[0]
    across = (((1,), (1,)), ((), ()))
    parts = parts_of(p)
    y = lax.dot_general(
        parts, act[...], across, preferred_element_type=jnp.float32
    )
    n = rank
    u = (y[2 * n : 3 * n] + y[n : 2 * n]) + y[:n]
    e, f, g = (
        lax.dot_general(
            parts, v.astype(jnp.bfloat16), across, preferred_element_type=jnp.float32
        )
        for v in three(feed[...])
    )
    small = (g[:n] + f[n : 2 * n]) + e[2 * n : 3 * n]
    err = (small + (f[:n] + e[n : 2 * n])) + e[:n]
    lane = lax.broadcasted_iota(jnp.int32, (rank, 128), 1)
    gram = jnp.zeros((rank, 128), jnp.float32)
    for i in range(rank):
        column = jnp.sum(p * p[i : i + 1], axis=1, keepdims=True)
        gram = jnp.where(lane == i, column, gram)
    for i in range(out.shape[0]):
        out[i, :, :toks] = u
        out[i, :, toks : toks + rows] = err
        out[i, :, toks + rows :] = gram


def hidden_kernel(got, hid, low, out, gram):
    toks, rows = hid.shape[1], out.shape[1] // 2
    u = total(got, slice(0, toks))
    err = total(got, slice(toks, toks + rows))
    gram[...] = total(got, slice(toks + rows, None))
    parts = parts_of(u)
    shard = lax.axis_index("x") * lax.axis_size("y") + lax.axis_index("y")
    mine = jnp.where(shard == lax.axis_index("z"), 1.0, 0.0)
    upper = jnp.where(lax.axis_index("c") == 0, mine, 0.0)
    lower = mine - upper
    n = out.shape[0]
    for i, (half, weight) in enumerate(((hid, upper), (low, lower))):
        y = lax.dot_general(
            parts,
            half[...],
            (((1,), (1,)), ((), ())),
            preferred_element_type=jnp.float32,
        )
        y = (y[2 * n : 3 * n] + y[n : 2 * n]) + y[:n]
        out[:, i * rows : (i + 1) * rows] = y + err * weight


def ranks_kernel(got, out):
    y = total(got, slice(None))
    part = out.shape[1]
    y = jnp.where(lax.axis_index("c") == 0, y[:part], y[part:])
    for i in range(out.shape[0]):
        out[i] = y


def half_kernel(got, out):
    rows = out.shape[2]
    y = total(got, slice(None))
    y = jnp.where(lax.axis_index("c") == 0, y[:, :rows], y[:, rows:])
    for i in range(out.shape[0]):
        out[i] = y


def block_kernel(got, inverse, out):
    rows = total(got, slice(None))
    inv = inverse[...]
    block = inv[:, 0:1] * rows[0:1]
    for i in range(1, rows.shape[0]):
        block = block + inv[:, i : i + 1] * rows[i : i + 1]
    block = block * (1.0 / out.shape[0])
    for i in range(out.shape[0]):
        out[i] = block


def last_kernel(
    blocks, ortho, base, momentum, feed_out, mom_out, q_out, feed_new, mom_new, sems
):
    count, _, rows = blocks.shape
    sends = []
    for i in range(count):
        there = q_out.at[:, pl.ds(i * rows, rows)]
        sends.append(pltpu.make_async_copy(blocks.at[i], there, sems.at[i]))
    for send in sends:
        send.start()
    replica = lax.axis_index("z") * lax.axis_size("c") + lax.axis_index("c")
    a, b, c = three(blocks[replica])
    left = jnp.concatenate([c, b, a, b, a, a], 0).astype(jnp.bfloat16)
    a, b, c = three(ortho[...])
    right = jnp.concatenate([a, b, c, a, b, a], 0).astype(jnp.bfloat16)
    part = feed_new.shape[0] // 3
    for i in range(3):
        piece = slice(i * part, (i + 1) * part)
        approx = lax.dot_general(
            left[:, piece],
            right,
            (((0,), (0,)), ((), ())),
            preferred_element_type=jnp.float32,
        )
        feed_new[piece] = base[piece] - approx
        mom_new[piece] = decay_rate * momentum[piece] + approx
        for j, (here, there) in enumerate(((feed_new, feed_out), (mom_new, mom_out))):
            span = pl.ds(i * part, part)
            send = pltpu.make_async_copy(
                here.at[span], there.at[span], sems.at[count + 2 * i + j]
            )
            send.start()
            sends.append(send)
    for send in sends:
        send.wait()


def tie(x, after):
    return lax.optimization_barrier((x, after))[0]


def tree_rounds(nz, nc, nx, ny):
    def device(z, c, x, y):
        return ((z * nc + c) * nx + x) * ny + y

    rounds = []
    known = {c: [(0, 0)] for c in range(nc)}
    steps = ((nx // 2, 0), (0, ny // 2), (nx // 4, 0), (0, ny // 4))
    for step in steps:
        pairs = []
        for c in range(nc):
            dx, dy = step if c == 0 else (step[1], step[0])
            fresh = [((a + dx) % nx, (b + dy) % ny) for a, b in known[c]]
            for z in range(nz):
                ox, oy = z // ny, z % ny
                for (a, b), (e, f) in zip(known[c], fresh):
                    source = device(z, c, (ox + a) % nx, (oy + b) % ny)
                    target = device(z, c, (ox + e) % nx, (oy + f) % ny)
                    pairs.append((source, target))
            known[c] = known[c] + fresh
        rounds.append(pairs)
    return rounds


def per_device(activations, hidden, feedback, momentum, q_start):
    nz, nc, nx, ny = (lax.axis_size(a) for a in ("z", "c", "x", "y"))
    plane = ("x", "y")
    n_dp, n_mp = nz * nc, nx * ny
    z, core = lax.axis_index("z"), lax.axis_index("c")
    replica = z * nc + core
    shard = lax.axis_index("x") * ny + lax.axis_index("y")
    rank = q_start.shape[1]
    cols_mp, toks = hidden.shape
    cols_dp = feedback.shape[0]
    width = activations.shape[1]
    own_start = replica * cols_dp
    root_dev = own_start // cols_mp
    rounds = tree_rounds(nz, nc, nx, ny)
    off_x = (lax.axis_index("x") - z // ny) % nx
    off_y = (lax.axis_index("y") - z % ny) % ny
    first = jnp.where(core == 0, off_x, off_y)
    second = jnp.where(core == 0, off_y, off_x)
    turn = jnp.where(first >= 2, 0, -1)
    turn = jnp.where(second >= 2, 1, turn)
    turn = jnp.where(first % 2 == 1, 2, turn)
    turn = jnp.where(second % 2 == 1, 3, turn)

    def send(held, k):
        return lax.ppermute(held, ("z", "c", "x", "y"), rounds[k])

    def take(held, got, k):
        return jnp.where(turn == k, got, held)

    q_rows = q_start.T
    f32 = jnp.float32
    whole = pl.BlockSpec(memory_space=pltpu.VMEM)
    far = pl.BlockSpec(memory_space=pltpu.HBM)
    token_part, q_owned, held = pl.pallas_call(
        start_kernel,
        out_shape=[
            pltpu.HBM((n_mp, rank, toks), f32),
            pltpu.VMEM((rank, cols_dp), f32),
            pltpu.VMEM((cols_dp, toks), hidden.dtype),
        ],
        in_specs=[far] * 2,
        out_specs=[far, whole, whole],
        scratch_shapes=[
            pltpu.VMEM((rank, cols_mp), f32),
            pltpu.VMEM(hidden.shape, hidden.dtype),
            pltpu.VMEM((rank, toks), f32),
            pltpu.SemaphoreType.DMA((5,)),
            pltpu.SemaphoreType.DMA((n_mp,)),
        ],
        compiler_params=pltpu.CompilerParams(vmem_limit_bytes=4 * 2**20),
        cost_estimate=pl.CostEstimate(
            flops=2 * 10**9, bytes_accessed=3 * 10**6, transcendentals=0
        ),
    )(
        pltpu.with_memory_space_constraint(q_rows, pltpu.HBM),
        pltpu.with_memory_space_constraint(hidden, pltpu.HBM),
    )
    feed_near = near(feedback)
    act_near = activations
    (p_err,) = local(
        early_kernel,
        [pltpu.VMEM((rank, width), f32)],
        1.5,
        near(q_owned),
        feed_near,
    )
    held = tie(held, p_err)
    got = send(held, 0)
    tokens = near(lax.all_to_all(token_part, plane, 0, 0))
    (p_part,) = local(
        left_kernel,
        [pltpu.VMEM((rank, width), f32)],
        1,
        tokens,
        near(act_near),
        near(p_err),
    )
    part = rank // nc
    (p_pair,) = local(
        ranks_kernel,
        [pltpu.VMEM((nz, part, width), f32)],
        1,
        near(lax.all_gather(p_part, "c")),
    )
    held = take(held, tie(got, p_pair), 0)
    got = send(held, 1)
    p_half = lax.all_to_all(p_pair, "z", 0, 0).sum(0)
    held = take(held, got, 1)
    got = send(held, 2)
    p_sum = lax.all_gather(p_half, "c", tiled=True)

    (packed,) = local(
        right_kernel,
        [pltpu.VMEM((n_mp, rank, toks + cols_dp + 128), f32)],
        2,
        near(p_sum),
        near(act_near),
        feed_near,
    )
    hid_late = tie(hidden, packed)
    hid_top, hid_low = hid_late[:cols_dp], hid_late[cols_dp:]
    packed = near(lax.all_to_all(packed, plane, 0, 0))
    hid, gram_mat = local(
        hidden_kernel,
        [pltpu.VMEM((rank, cols_mp), f32), pltpu.VMEM((rank, 128), f32)],
        1,
        packed,
        near(hid_top),
        near(hid_low),
    )
    gram_mat = gram_mat[:, :rank]
    (half,) = local(
        half_kernel,
        [pltpu.VMEM((nz, rank, cols_dp), f32)],
        1,
        near(lax.all_gather(hid, "c")),
    )
    held = take(held, tie(got, half), 2)
    got = send(held, 3)
    gram_mat = tie(gram_mat, held)
    factor = jnp.linalg.cholesky(gram_mat)
    inverse = lax.linalg.triangular_solve(
        factor, jnp.eye(rank, dtype=jnp.float32), left_side=True, lower=True
    )
    half = near(lax.all_to_all(half, "z", 0, 0))
    (block,) = local(
        block_kernel,
        [pltpu.VMEM((n_dp, rank, cols_dp), f32)],
        1,
        half,
        near(inverse),
    )
    held = take(held, tie(got, block), 3)
    own_grad = jnp.dot(held, act_near, preferred_element_type=jnp.float32)
    base = lax.optimization_barrier(own_grad + feedback)
    blocks = near(lax.all_to_all(block, ("x", "y", "c"), 0, 0))
    ortho = jnp.dot(inverse, p_sum, precision=high)
    new_feedback, new_momentum, q_next = pl.pallas_call(
        last_kernel,
        out_shape=[
            pltpu.HBM(feedback.shape, f32),
            pltpu.HBM(momentum.shape, f32),
            pltpu.HBM(q_rows.shape, f32),
        ],
        in_specs=[whole] * 4,
        out_specs=[far] * 3,
        scratch_shapes=[
            pltpu.VMEM(feedback.shape, f32),
            pltpu.VMEM(momentum.shape, f32),
            pltpu.SemaphoreType.DMA((n_dp + 6,)),
        ],
        compiler_params=pltpu.CompilerParams(vmem_limit_bytes=4 * 2**20),
        cost_estimate=pl.CostEstimate(
            flops=2 * 10**9, bytes_accessed=3 * 10**6, transcendentals=0
        ),
    )(blocks, near(ortho), near(base), near(momentum))
    return (new_feedback, new_momentum, q_next.T)


def solution(mesh):
    grid = Mesh(mesh.devices.reshape(16, 2, 4, 4), ("z", "c", "x", "y"))
    dp, mp = ("z", "c"), ("x", "y")
    placed = (P(dp, mp), P(mp, dp), P(dp, mp), P(dp, mp), P())
    return jax.shard_map(
        per_device,
        mesh=grid,
        in_specs=placed,
        out_specs=(P(dp, mp), P(dp, mp), P()),
        check_vma=False,
    )
```

```python
import jax
import jax.numpy as jnp
from jax import lax
from jax.experimental import pallas as pl
from jax.experimental.pallas import tpu as pltpu
from jax.sharding import Mesh, PartitionSpec as P

decay_rate = 0.9
high = lax.Precision.HIGHEST


def copies(x, axes, count):
    return lax.all_to_all(jnp.broadcast_to(x[None], (count,) + x.shape), axes, 0, 0)


def near(x):
    return pltpu.with_memory_space_constraint(x, pltpu.VMEM)


def local(kernel, outs, micros, *args):
    whole = pl.BlockSpec(memory_space=pltpu.VMEM)
    size = sum(a.size * a.dtype.itemsize for a in args)
    return pl.pallas_call(
        kernel,
        out_shape=outs,
        in_specs=[whole] * len(args),
        out_specs=[whole] * len(outs),
        compiler_params=pltpu.CompilerParams(vmem_limit_bytes=4 * 2**20),
        cost_estimate=pl.CostEstimate(
            flops=int(micros * 4e9), bytes_accessed=size, transcendentals=0
        ),
    )(*args)


def exact_dot(x, wide, dims):
    y = lax.dot_general(
        parts_of(x), wide, (dims, ((), ())), preferred_element_type=jnp.float32
    )
    n = x.shape[0]
    return (y[2 * n : 3 * n] + y[n : 2 * n]) + y[:n]


def total(ref, lanes):
    y = ref[0, :, lanes]
    for i in range(1, ref.shape[0]):
        y = y + ref[i, :, lanes]
    return y


def three(x):
    a = x.astype(jnp.bfloat16).astype(jnp.float32)
    r = x - a
    b = r.astype(jnp.bfloat16).astype(jnp.float32)
    return a, b, r - b


def parts_of(x):
    return jnp.concatenate([*three(x), jnp.zeros_like(x)], 0).astype(jnp.bfloat16)


def start_kernel(q, hid, out, q_own, piece_out, q_near, held, row, sems, done):
    rows, own_rows = hid.shape[0], q_own.shape[1]
    count = sems.shape[0] - 2
    step = rows // count
    shard = lax.axis_index("x") * lax.axis_size("y") + lax.axis_index("y")
    replica = lax.axis_index("z") * lax.axis_size("c") + lax.axis_index("c")
    mine = q.at[:, pl.ds(pl.multiple_of(shard * rows, rows), rows)]
    own = q.at[:, pl.ds(pl.multiple_of(replica * own_rows, own_rows), own_rows)]
    first = pltpu.make_async_copy(mine, q_near, sems.at[count])
    last = pltpu.make_async_copy(own, q_own, sems.at[count + 1])
    loads = []
    for i in range(count):
        piece = pl.ds(i * step, step)
        loads.append(pltpu.make_async_copy(hid.at[piece], held.at[piece], sems.at[i]))
    for load in [first] + loads + [last]:
        load.start()
    first.wait()
    parts = parts_of(q_near[...])
    y = jnp.zeros((parts.shape[0], hid.shape[1]), jnp.float32)
    for i in range(count):
        loads[i].wait()
        y = y + jnp.dot(
            parts[:, i * step : (i + 1) * step],
            held[i * step : (i + 1) * step, :],
            preferred_element_type=jnp.float32,
        )
    n = row.shape[0]
    row[...] = (y[2 * n : 3 * n] + y[n : 2 * n]) + y[:n]
    sends = [
        pltpu.make_async_copy(row, out.at[i], done.at[i]) for i in range(out.shape[0])
    ]
    for send in sends:
        send.start()
    core = lax.axis_index("c")
    piece_out[...] = held[pl.ds(pl.multiple_of(core * own_rows, own_rows), own_rows), :]
    last.wait()
    for send in sends:
        send.wait()


def early_kernel(q, feed, err):
    err[...] = jnp.dot(
        q[...], feed[...], precision=high, preferred_element_type=jnp.float32
    )


def left_kernel(got, act, err, out):
    tokens = total(got, slice(None))
    out[...] = exact_dot(tokens, act[...], ((1,), (0,))) + err[...]


def right_kernel(p_ref, act, feed, out):
    p = p_ref[...]
    rank, toks = p.shape[0], act.shape[0]
    rows = feed.shape[0]
    across = (((1,), (1,)), ((), ()))
    parts = parts_of(p)
    y = lax.dot_general(
        parts, act[...], across, preferred_element_type=jnp.float32
    )
    n = rank
    u = (y[2 * n : 3 * n] + y[n : 2 * n]) + y[:n]
    e, f, g = (
        lax.dot_general(
            parts, v.astype(jnp.bfloat16), across, preferred_element_type=jnp.float32
        )
        for v in three(feed[...])
    )
    small = (g[:n] + f[n : 2 * n]) + e[2 * n : 3 * n]
    err = (small + (f[:n] + e[n : 2 * n])) + e[:n]
    lane = lax.broadcasted_iota(jnp.int32, (rank, 128), 1)
    gram = jnp.zeros((rank, 128), jnp.float32)
    for i in range(rank):
        column = jnp.sum(p * p[i : i + 1], axis=1, keepdims=True)
        gram = jnp.where(lane == i, column, gram)
    for i in range(out.shape[0]):
        out[i, :, :toks] = u
        out[i, :, toks : toks + rows] = err
        out[i, :, toks + rows :] = gram


def hidden_kernel(got, hid, low, out, gram):
    toks, rows = hid.shape[1], out.shape[1] // 2
    u = total(got, slice(0, toks))
    err = total(got, slice(toks, toks + rows))
    gram[...] = total(got, slice(toks + rows, None))
    parts = parts_of(u)
    shard = lax.axis_index("x") * lax.axis_size("y") + lax.axis_index("y")
    mine = jnp.where(shard == lax.axis_index("z"), 1.0, 0.0)
    upper = jnp.where(lax.axis_index("c") == 0, mine, 0.0)
    lower = mine - upper
    n = out.shape[0]
    for i, (half, weight) in enumerate(((hid, upper), (low, lower))):
        y = lax.dot_general(
            parts,
            half[...],
            (((1,), (1,)), ((), ())),
            preferred_element_type=jnp.float32,
        )
        y = (y[2 * n : 3 * n] + y[n : 2 * n]) + y[:n]
        out[:, i * rows : (i + 1) * rows] = y + err * weight


def ranks_kernel(got, out):
    y = total(got, slice(None))
    part = out.shape[1]
    y = jnp.where(lax.axis_index("c") == 0, y[:part], y[part:])
    for i in range(out.shape[0]):
        out[i] = y


def half_kernel(got, out):
    rows = out.shape[2]
    y = total(got, slice(None))
    y = jnp.where(lax.axis_index("c") == 0, y[:, :rows], y[:, rows:])
    for i in range(out.shape[0]):
        out[i] = y


def block_kernel(got, inverse, out):
    rows = total(got, slice(None))
    inv = inverse[...]
    block = inv[:, 0:1] * rows[0:1]
    for i in range(1, rows.shape[0]):
        block = block + inv[:, i : i + 1] * rows[i : i + 1]
    block = block * (1.0 / out.shape[0])
    for i in range(out.shape[0]):
        out[i] = block


def last_kernel(
    blocks, ortho, base, momentum, feed_out, mom_out, q_out, feed_new, mom_new, q_new, sems
):
    count, _, rows = blocks.shape
    sends = []
    group = count // 4
    for i in range(count):
        q_new[:, i * rows : (i + 1) * rows] = blocks[i]
        if (i + 1) % group == 0:
            span = pl.ds((i + 1 - group) * rows, group * rows)
            send = pltpu.make_async_copy(
                q_new.at[:, span], q_out.at[:, span], sems.at[i // group]
            )
            send.start()
            sends.append(send)
    replica = lax.axis_index("z") * lax.axis_size("c") + lax.axis_index("c")
    a, b, c = three(blocks[replica])
    left = jnp.concatenate([c, b, a, b, a, a], 0).astype(jnp.bfloat16)
    a, b, c = three(ortho[...])
    right = jnp.concatenate([a, b, c, a, b, a], 0).astype(jnp.bfloat16)
    part = feed_new.shape[0] // 3
    for i in range(3):
        piece = slice(i * part, (i + 1) * part)
        approx = lax.dot_general(
            left[:, piece],
            right,
            (((0,), (0,)), ((), ())),
            preferred_element_type=jnp.float32,
        )
        feed_new[piece] = base[piece] - approx
        mom_new[piece] = decay_rate * momentum[piece] + approx
        for j, (here, there) in enumerate(((feed_new, feed_out), (mom_new, mom_out))):
            span = pl.ds(i * part, part)
            send = pltpu.make_async_copy(
                here.at[span], there.at[span], sems.at[4 + 2 * i + j]
            )
            send.start()
            sends.append(send)
    for send in sends:
        send.wait()


def tie(x, after):
    return lax.optimization_barrier((x, after))[0]


def tree_rounds(nz, nc, nx, ny):
    def device(z, c, x, y):
        return ((z * nc + c) * nx + x) * ny + y

    rounds = []
    known = {c: [(0, 0)] for c in range(nc)}
    steps = ((nx // 2, 0), (0, ny // 2), (nx // 4, 0), (0, ny // 4))
    for step in steps:
        pairs = []
        for c in range(nc):
            dx, dy = step if c == 0 else (step[1], step[0])
            fresh = [((a + dx) % nx, (b + dy) % ny) for a, b in known[c]]
            for z in range(nz):
                ox, oy = z // ny, z % ny
                for (a, b), (e, f) in zip(known[c], fresh):
                    source = device(z, c, (ox + a) % nx, (oy + b) % ny)
                    target = device(z, c, (ox + e) % nx, (oy + f) % ny)
                    pairs.append((source, target))
            known[c] = known[c] + fresh
        rounds.append(pairs)
    return rounds


def per_device(activations, hidden, feedback, momentum, q_start):
    nz, nc, nx, ny = (lax.axis_size(a) for a in ("z", "c", "x", "y"))
    plane = ("x", "y")
    n_dp, n_mp = nz * nc, nx * ny
    z, core = lax.axis_index("z"), lax.axis_index("c")
    replica = z * nc + core
    shard = lax.axis_index("x") * ny + lax.axis_index("y")
    rank = q_start.shape[1]
    cols_mp, toks = hidden.shape
    cols_dp = feedback.shape[0]
    width = activations.shape[1]
    own_start = replica * cols_dp
    root_dev = own_start // cols_mp
    rounds = tree_rounds(nz, nc, nx, ny)
    off_x = (lax.axis_index("x") - z // ny) % nx
    off_y = (lax.axis_index("y") - z % ny) % ny
    first = jnp.where(core == 0, off_x, off_y)
    second = jnp.where(core == 0, off_y, off_x)
    turn = jnp.where(first >= 2, 0, -1)
    turn = jnp.where(second >= 2, 1, turn)
    turn = jnp.where(first % 2 == 1, 2, turn)
    turn = jnp.where(second % 2 == 1, 3, turn)

    def send(held, k):
        return lax.ppermute(held, ("z", "c", "x", "y"), rounds[k])

    def take(held, got, k):
        return jnp.where(turn == k, got, held)

    q_rows = q_start.T
    f32 = jnp.float32
    whole = pl.BlockSpec(memory_space=pltpu.VMEM)
    far = pl.BlockSpec(memory_space=pltpu.HBM)
    token_part, q_owned, held = pl.pallas_call(
        start_kernel,
        out_shape=[
            pltpu.HBM((n_mp, rank, toks), f32),
            pltpu.VMEM((rank, cols_dp), f32),
            pltpu.VMEM((cols_dp, toks), hidden.dtype),
        ],
        in_specs=[far] * 2,
        out_specs=[far, whole, whole],
        scratch_shapes=[
            pltpu.VMEM((rank, cols_mp), f32),
            pltpu.VMEM(hidden.shape, hidden.dtype),
            pltpu.VMEM((rank, toks), f32),
            pltpu.SemaphoreType.DMA((5,)),
            pltpu.SemaphoreType.DMA((n_mp,)),
        ],
        compiler_params=pltpu.CompilerParams(vmem_limit_bytes=4 * 2**20),
        cost_estimate=pl.CostEstimate(
            flops=2 * 10**9, bytes_accessed=3 * 10**6, transcendentals=0
        ),
    )(
        pltpu.with_memory_space_constraint(q_rows, pltpu.HBM),
        pltpu.with_memory_space_constraint(hidden, pltpu.HBM),
    )
    feed_near = near(feedback)
    act_near = activations
    (p_err,) = local(
        early_kernel,
        [pltpu.VMEM((rank, width), f32)],
        1.5,
        near(q_owned),
        feed_near,
    )
    held = tie(held, p_err)
    got = send(held, 0)
    tokens = near(lax.all_to_all(token_part, plane, 0, 0))
    (p_part,) = local(
        left_kernel,
        [pltpu.VMEM((rank, width), f32)],
        1,
        tokens,
        near(act_near),
        near(p_err),
    )
    part = rank // nc
    (p_pair,) = local(
        ranks_kernel,
        [pltpu.VMEM((nz, part, width), f32)],
        1,
        near(lax.all_gather(p_part, "c")),
    )
    held = take(held, tie(got, p_pair), 0)
    got = send(held, 1)
    p_half = lax.all_to_all(p_pair, "z", 0, 0).sum(0)
    held = take(held, got, 1)
    got = send(held, 2)
    p_sum = lax.all_gather(p_half, "c", tiled=True)

    (packed,) = local(
        right_kernel,
        [pltpu.VMEM((n_mp, rank, toks + cols_dp + 128), f32)],
        2,
        near(p_sum),
        near(act_near),
        feed_near,
    )
    hid_late = tie(hidden, packed)
    hid_top, hid_low = hid_late[:cols_dp], hid_late[cols_dp:]
    packed = near(lax.all_to_all(packed, plane, 0, 0))
    hid, gram_mat = local(
        hidden_kernel,
        [pltpu.VMEM((rank, cols_mp), f32), pltpu.VMEM((rank, 128), f32)],
        1,
        packed,
        near(hid_top),
        near(hid_low),
    )
    gram_mat = gram_mat[:, :rank]
    (half,) = local(
        half_kernel,
        [pltpu.VMEM((nz, rank, cols_dp), f32)],
        1,
        near(lax.all_gather(hid, "c")),
    )
    held = take(held, tie(got, half), 2)
    got = send(held, 3)
    gram_mat = tie(gram_mat, held)
    factor = jnp.linalg.cholesky(gram_mat)
    inverse = lax.linalg.triangular_solve(
        factor, jnp.eye(rank, dtype=jnp.float32), left_side=True, lower=True
    )
    half = near(lax.all_to_all(half, "z", 0, 0))
    (block,) = local(
        block_kernel,
        [pltpu.VMEM((n_dp, rank, cols_dp), f32)],
        1,
        half,
        near(inverse),
    )
    held = take(held, tie(got, block), 3)
    own_grad = jnp.dot(held, act_near, preferred_element_type=jnp.float32)
    base = lax.optimization_barrier(own_grad + feedback)
    blocks = near(lax.all_to_all(block, ("x", "y", "c"), 0, 0))
    ortho = jnp.dot(inverse, p_sum, precision=high)
    new_feedback, new_momentum, q_next = pl.pallas_call(
        last_kernel,
        out_shape=[
            pltpu.HBM(feedback.shape, f32),
            pltpu.HBM(momentum.shape, f32),
            pltpu.HBM(q_rows.shape, f32),
        ],
        in_specs=[whole] * 4,
        out_specs=[far] * 3,
        scratch_shapes=[
            pltpu.VMEM(feedback.shape, f32),
            pltpu.VMEM(momentum.shape, f32),
            pltpu.VMEM(q_rows.shape, f32),
            pltpu.SemaphoreType.DMA((10,)),
        ],
        compiler_params=pltpu.CompilerParams(vmem_limit_bytes=4 * 2**20),
        cost_estimate=pl.CostEstimate(
            flops=2 * 10**9, bytes_accessed=3 * 10**6, transcendentals=0
        ),
    )(blocks, near(ortho), near(base), near(momentum))
    return (new_feedback, new_momentum, q_next.T)


def solution(mesh):
    grid = Mesh(mesh.devices.reshape(16, 2, 4, 4), ("z", "c", "x", "y"))
    dp, mp = ("z", "c"), ("x", "y")
    placed = (P(dp, mp), P(mp, dp), P(dp, mp), P(dp, mp), P())
    return jax.shard_map(
        per_device,
        mesh=grid,
        in_specs=placed,
        out_specs=(P(dp, mp), P(dp, mp), P()),
        check_vma=False,
    )
```
